128 devices in a mesh: span: 16 (over z, x_hi, core), vert: 8 (over y, x_lo).
Axes of the slice: x: 4 (x_hi: 2, x_lo: 2; x = x_hi * 2 + x_lo), y: 4, z: 4, core: 2. Of those that a mesh axis runs over, the one named last changes fastest.
Arguments:
- adjoint: float32 [19, 128, 128, 1024], P(None, 'span', 'vert'), may hold values from -6 to 6
- saved: bfloat16 [19, 128, 128, 1024], P(None, 'span', 'vert')
- solid: int32 [128, 128, 1024], P('span', 'vert'), may hold values 0 or 1
- send_cells: int32 [128, 128, 128], P(('span', 'vert')), may hold values from 0 to 131071
- send_dirs: int32 [128, 128, 128], P(('span', 'vert')), may hold values from 1 to 18
- send_weight: float32 [128, 128, 128], P(('span', 'vert')), may hold values from 0.5 to 2
- send_counts: int32 [128, 128], P(('span', 'vert')), may hold values from 0 to 128, as said below
- recv_slots: int32 [128, 128, 128], P(('span', 'vert')), may hold values from 0 to 4095
Outputs:
- adjoint_prev: float32 [19, 128, 128, 1024], P(None, 'span', 'vert')
- element_sens: float32 [524288], P(('span', 'vert'))
The draws below stay inside these ranges and needn't reach their ends.
Inputs may be any that keep to these rules, and one draw needn't show every extreme that they name: `send_counts`: every device sends exactly 128 live links to one owner.
All inputs are finite; a program needn't handle non-finite values. No bound on the sum of `solid` on one device may be relied on, other than what follows from the above.
Results may differ from the reference program's by a relative error of at most 0.0003.
Values sent between devices are 32-bit elements; how exact they have to be, the bound alone decides.
No kernel may reach another device: no remote copies, remote signals or barrier semaphores. Data moves between devices by JAX's collectives and lax.ppermute only.
A program may use at most 192 MiB of HBM per device.

```python
import jax
import jax.numpy as jnp

Q = 19
CS = 8
CV = 16
NX = 1024
CAP = 128
ELEM_DEV = 4096
OWNERS = 128
NS = 128
NV = 128
N_SPAN = 16
N_VERT = 8


LATTICE_WEIGHTS = [1.0 / 3.0] + [1.0 / 18.0] * 6 + [1.0 / 36.0] * 12


LATTICE_VECS = [(0, 0, 0), (1, 0, 0), (-1, 0, 0), (0, 1, 0), (0, -1, 0), (0, 0, 1), (0, 0, -1), (1, 1, 0), (-1, -1, 0), (1, -1, 0), (-1, 1, 0), (1, 0, 1), (-1, 0, -1), (1, 0, -1), (-1, 0, 1), (0, 1, 1), (0, -1, -1), (0, 1, -1), (0, -1, 1)]


def equilibrium(key_rho, key_flow, rho_lo, rho_hi, mean_flow, flow_spread, noise):
    table = jnp.array(LATTICE_WEIGHTS, jnp.float32).reshape(19, 1, 1, 1)
    span_tab = jnp.array([c[0] for c in LATTICE_VECS], jnp.float32).reshape(19, 1, 1, 1)
    vert_tab = jnp.array([c[1] for c in LATTICE_VECS], jnp.float32).reshape(19, 1, 1, 1)
    strm_tab = jnp.array([c[2] for c in LATTICE_VECS], jnp.float32).reshape(19, 1, 1, 1)
    rho = jax.random.uniform(key_rho, (1, NS, NV, NX), jnp.float32, rho_lo, rho_hi)
    flow = flow_spread * jax.random.uniform(key_flow, (3, NS, NV, NX), jnp.float32, -1.0, 1.0)
    vel_s = flow[0:1]
    vel_v = flow[1:2]
    vel_x = mean_flow + flow[2:3]
    cu = span_tab * vel_s + vert_tab * vel_v + strm_tab * vel_x
    usq = vel_s * vel_s + vel_v * vel_v + vel_x * vel_x
    equil = table * rho * (1.0 + 3.0 * cu + 4.5 * cu * cu - 1.5 * usq)
    return equil * (1.0 + noise)


def draw_saved(key, part):
    key = jax.random.fold_in(key, 1)
    key_rho, key_flow, key_noise = jax.random.split(key, 3)
    noise = jax.random.uniform(key_noise, (19, NS, NV, NX), jnp.float32, -0.2, 0.2)
    result = equilibrium(key_rho, key_flow, 0.9, 1.1, 0.06, 0.04, noise)
    return result.astype(jnp.bfloat16)


def draw_send_counts(key, part):
    key = jax.random.fold_in(key, 2)
    key_base, key_div, key_shift = jax.random.split(key, 3)
    owners = N_SPAN * N_VERT
    base = jax.random.randint(key_base, (owners, owners), CAP // 2, CAP + 1)
    divisor = jax.random.randint(key_div, (owners, 1), 1, 3)
    counts = base // divisor
    offset = jax.random.randint(key_shift, (), 0, owners)
    rows = jnp.arange(owners, dtype=jnp.int32)[:, None]
    cols = jnp.arange(owners, dtype=jnp.int32)[None, :]
    full = cols == (rows + offset) % owners
    return jnp.where(full, CAP, counts).astype(jnp.int32)


def with_ends(values, own_key, least, high):
    spot = [jax.random.randint(jax.random.fold_in(own_key, axis), (), 0, length) for axis, length in enumerate(values.shape)]
    main_axis = values.shape.index(max(values.shape))
    beside = spot[:main_axis] + [(spot[main_axis] + 1) % values.shape[main_axis]] + spot[main_axis + 1:]
    return values.at[tuple(spot)].set(least).at[tuple(beside)].set(high)


def shard_levels(stream_key, extent, cuts, smallest, top_value):
    gain = 1.0
    for axis_at, blocks in cuts:
        heights = jax.random.uniform(jax.random.fold_in(jax.random.fold_in(stream_key, 6), axis_at), (blocks,), jnp.float32, smallest / len(cuts), top_value / len(cuts))
        gain = gain * jnp.repeat(jnp.exp(heights), extent[axis_at] // blocks).reshape((-1,) + (1,) * (len(extent) - 1 - axis_at))
    return gain


def centred(stream_key, shape, deviation, limit, cuts=(), kind=jnp.bfloat16):
    entries = deviation * jax.random.normal(stream_key, shape, jnp.float32)
    if cuts:
        entries = entries * shard_levels(stream_key, shape, cuts, -0.22, 0.18)
    return jnp.clip(entries, -limit, limit).astype(kind)


def setup_inputs(seed: int = 0) -> dict:
    key_list = jax.random.split(jax.random.key(seed), 9)
    adjoint = centred(key_list[0], (Q, NS, NV, NX), 1.0, 6.0, ((1, 16), (2, 8)), jnp.float32)
    saved = draw_saved(jax.random.fold_in(key_list[8], 71), 0)
    solid = with_ends((jax.random.randint(key_list[2], (NS, NV, NX), 0, 4) < 1).astype(jnp.int32), jax.random.fold_in(key_list[2], 1), 0, 1)
    send_cells = with_ends(jax.random.randint(key_list[3], (OWNERS, OWNERS, CAP), 0, CS * CV * NX), jax.random.fold_in(key_list[3], 1), 0, (CS * CV * NX) - 1).astype(jnp.int32)
    send_dirs = with_ends(jax.random.randint(key_list[4], (OWNERS, OWNERS, CAP), 1, 19), jax.random.fold_in(key_list[4], 1), 1, 18).astype(jnp.int32)
    send_weight = jnp.clip(0.5 + 1.5 * jax.random.uniform(key_list[5], (OWNERS, OWNERS, CAP), jnp.float32) ** shard_levels(key_list[5], (OWNERS, OWNERS, CAP), ((0, 128),), -0.2, 0.2), 0.5, 2.0)
    send_counts = draw_send_counts(jax.random.fold_in(key_list[8], 71), 0)
    recv_slots = with_ends(jax.random.randint(key_list[7], (OWNERS, OWNERS, CAP), 0, ELEM_DEV), jax.random.fold_in(key_list[7], 1), 0, ELEM_DEV - 1).astype(jnp.int32)
    return {"adjoint": adjoint, "saved": saved, "solid": solid, "send_cells": send_cells, "send_dirs": send_dirs, "send_weight": send_weight, "send_counts": send_counts, "recv_slots": recv_slots}


VECS = [(0, 0, 0), (1, 0, 0), (-1, 0, 0), (0, 1, 0), (0, -1, 0), (0, 0, 1), (0, 0, -1),
        (1, 1, 0), (-1, -1, 0), (1, -1, 0), (-1, 1, 0), (1, 0, 1), (-1, 0, -1),
        (1, 0, -1), (-1, 0, 1), (0, 1, 1), (0, -1, -1), (0, 1, -1), (0, -1, 1)]
WEIGHTS = [1.0 / 3.0] + [1.0 / 18.0] * 6 + [1.0 / 36.0] * 12
OPPOSITE = [0, 2, 1, 4, 3, 6, 5, 8, 7, 10, 9, 12, 11, 14, 13, 16, 15, 18, 17]
OMEGA = 1.6


def stream(extended, rows_s, rows_v):
    pieces = []
    for i in range(19):
        cs, cv, cx = VECS[i]
        piece = extended[i, 1 + cs:1 + cs + rows_s, 1 + cv:1 + cv + rows_v, :]
        pieces.append(jnp.roll(piece, -cx, axis=-1))
    return jnp.stack(pieces, 0)


def collide(pulled, saved, solid):
    popul = saved.astype(jnp.float32)
    rho = popul[0]
    mom_s = jnp.zeros_like(rho)
    mom_v = jnp.zeros_like(rho)
    mom_x = jnp.zeros_like(rho)
    for i in range(1, 19):
        rho = rho + popul[i]
        cs, cv, cx = VECS[i]
        if cs != 0:
            mom_s = mom_s + cs * popul[i]
        if cv != 0:
            mom_v = mom_v + cv * popul[i]
        if cx != 0:
            mom_x = mom_x + cx * popul[i]
    vel_s = mom_s / rho
    vel_v = mom_v / rho
    vel_x = mom_x / rho
    usq = vel_s * vel_s + vel_v * vel_v + vel_x * vel_x
    g_rho = jnp.zeros_like(rho)
    g_s = jnp.zeros_like(rho)
    g_v = jnp.zeros_like(rho)
    g_x = jnp.zeros_like(rho)
    for i in range(19):
        cs, cv, cx = VECS[i]
        cu = cs * vel_s + cv * vel_v + cx * vel_x
        weighted = WEIGHTS[i] * pulled[i]
        g_rho = g_rho + weighted * (1.0 - 4.5 * cu * cu + 1.5 * usq)
        g_s = g_s + weighted * (3.0 * cs + 9.0 * cu * cs - 3.0 * vel_s)
        g_v = g_v + weighted * (3.0 * cv + 9.0 * cu * cv - 3.0 * vel_v)
        g_x = g_x + weighted * (3.0 * cx + 9.0 * cu * cx - 3.0 * vel_x)
    is_solid = solid == 1
    result = []
    for j in range(19):
        cs, cv, cx = VECS[j]
        fluid_term = (1.0 - OMEGA) * pulled[j] + OMEGA * (g_rho + cs * g_s + cv * g_v + cx * g_x)
        result.append(jnp.where(is_solid, pulled[OPPOSITE[j]], fluid_term))
    return jnp.stack(result, 0)


def opposite_of(dirs):
    return jnp.where(dirs == 0, 0, jnp.where(dirs % 2 == 1, dirs + 1, dirs - 1)).astype(jnp.int32)


def link_terms(brick, cells, dirs, weight, counts):
    picked = brick[dirs, cells] - brick[opposite_of(dirs), cells]
    live = jnp.arange(cells.shape[-1], dtype=jnp.int32)[None, :] < counts[:, None]
    return jnp.where(live, weight * picked, jnp.float32(0.0))


def reference(adjoint, saved, solid, send_cells, send_dirs, send_weight, send_counts, recv_slots):
    wrapped = jnp.concatenate([adjoint[:, -1:], adjoint, adjoint[:, :1]], axis=1)
    extended = jnp.pad(wrapped, ((0, 0), (0, 0), (1, 1), (0, 0)))
    pulled = stream(extended, NS, NV)
    bricks = pulled.reshape(19, N_SPAN, CS, N_VERT, CV, NX).transpose(1, 3, 0, 2, 4, 5)
    bricks = bricks.reshape(N_SPAN * N_VERT, 19, CS * CV * NX)
    values = jax.vmap(link_terms)(bricks, send_cells, send_dirs, send_weight, send_counts)
    owners = N_SPAN * N_VERT
    owner_idx = jnp.broadcast_to(jnp.arange(owners, dtype=jnp.int32)[:, None, None], recv_slots.shape)
    sens = jnp.zeros((owners, ELEM_DEV), jnp.float32).at[owner_idx, recv_slots].add(values.transpose(1, 0, 2))
    adjoint_prev = collide(pulled, saved, solid)
    return adjoint_prev, sens.reshape(owners * ELEM_DEV)
```

```python
import jax
import jax.numpy as jnp
from jax import lax
from jax.experimental import pallas as pl
from jax.experimental.pallas import tpu as pltpu
from jax.sharding import PartitionSpec as P

Q = 19
CS = 8
CV = 16
NX = 1024
CAP = 128
OWNERS = 128
ELEM_DEV = 4096
PAIRS = 9
LANES = 128
COLS = NX // LANES
ROWS = PAIRS * CS * CV * COLS
OMEGA = 1.6

VECS = [
    (0, 0, 0),
    (1, 0, 0),
    (-1, 0, 0),
    (0, 1, 0),
    (0, -1, 0),
    (0, 0, 1),
    (0, 0, -1),
    (1, 1, 0),
    (-1, -1, 0),
    (1, -1, 0),
    (-1, 1, 0),
    (1, 0, 1),
    (-1, 0, -1),
    (1, 0, -1),
    (-1, 0, 1),
    (0, 1, 1),
    (0, -1, -1),
    (0, 1, -1),
    (0, -1, 1),
]
SPAN_UP = [i for i in range(Q) if VECS[i][0] == 1]
SPAN_DOWN = [i for i in range(Q) if VECS[i][0] == -1]
VERT_UP = [i for i in range(Q) if VECS[i][1] == 1]
VERT_DOWN = [i for i in range(Q) if VECS[i][1] == -1]

VMEM = pl.BlockSpec(memory_space=pltpu.VMEM)
SMEM = pl.BlockSpec(memory_space=pltpu.SMEM)
ANY = pl.BlockSpec(memory_space=pl.ANY)


def collide(pulled, sums, diffs, saved, is_solid, store):
    f = [saved(i) for i in range(Q)]
    e = [None] * PAIRS
    o = [None] * PAIRS
    for p in range(PAIRS):
        e[p] = f[2 * p + 1] + f[2 * p + 2]
        o[p] = f[2 * p + 1] - f[2 * p + 2]
    rho = f[0] + ((e[0] + e[1]) + (e[2] + e[3])) + ((e[4] + e[5]) + (e[6] + e[7]) + e[8])
    us = (o[0] + ((o[3] + o[4]) + (o[5] + o[6]))) / rho
    uv = (o[1] + ((o[3] - o[4]) + (o[7] + o[8]))) / rho
    ux = (o[2] + ((o[5] - o[6]) + (o[7] - o[8]))) / rho
    usq = us * us + uv * uv + ux * ux
    d0, d1, d2, d3, d4, d5, d6, d7, d8 = diffs
    s0, s1, s2, s3, s4, s5, s6, s7, s8 = sums
    w = 1.0 / 36.0
    s34 = s3 + s4
    s56 = s5 + s6
    s78 = s7 + s8
    two0 = 2.0 * s0
    two1 = 2.0 * s1
    two2 = 2.0 * s2
    m0 = 12.0 * pulled[0] + (two0 + two1 + two2) + (s34 + s56 + s78)
    mss = two0 + s34 + s56
    mvv = two1 + s34 + s78
    mxx = two2 + s56 + s78
    msv = s3 - s4
    msx = s5 - s6
    mvx = s7 - s8
    ms = 2.0 * d0 + ((d3 + d4) + (d5 + d6))
    mv = 2.0 * d1 + ((d3 - d4) + (d7 + d8))
    mx = 2.0 * d2 + ((d5 - d6) + (d7 - d8))
    as_ = mss * us + msv * uv + msx * ux
    av = msv * us + mvv * uv + mvx * ux
    ax = msx * us + mvx * uv + mxx * ux
    k = OMEGA * w
    g = (k * m0) * (1.0 + 1.5 * usq) - (4.5 * k) * (us * as_ + uv * av + ux * ax)
    gs = (3.0 * k) * ((ms + 3.0 * as_) - us * m0)
    gv = (3.0 * k) * ((mv + 3.0 * av) - uv * m0)
    gx = (3.0 * k) * ((mx + 3.0 * ax) - ux * m0)
    keep = 1.0 - OMEGA
    store(0, jnp.where(is_solid, pulled[0], keep * pulled[0] + g))
    along = [gs, gv, gx, gs + gv, gs - gv, gs + gx, gs - gx, gv + gx, gv - gx]
    for p in range(PAIRS):
        a = pulled[2 * p + 1]
        b = pulled[2 * p + 2]
        store(2 * p + 1, jnp.where(is_solid, b, keep * a + (g + along[p])))
        store(2 * p + 2, jnp.where(is_solid, a, keep * b + (g - along[p])))


def load_copies(adj, h_up, h_dn, wide, sem):
    copies = []
    for lo, hi in ((0, 1), (3, 7), (15, 19)):
        copies.append(pltpu.make_async_copy(adj.at[pl.ds(lo, hi - lo)], wide.at[pl.ds(lo, hi - lo)], sem.at[len(copies)]))
    for k, i in enumerate(SPAN_UP):
        copies.append(pltpu.make_async_copy(adj.at[i, pl.ds(1, CS - 1)], wide.at[i, pl.ds(0, CS - 1)], sem.at[len(copies)]))
        copies.append(pltpu.make_async_copy(h_up.at[k], wide.at[i, CS - 1], sem.at[len(copies)]))
    for k, i in enumerate(SPAN_DOWN):
        copies.append(pltpu.make_async_copy(adj.at[i, pl.ds(0, CS - 1)], wide.at[i, pl.ds(1, CS - 1)], sem.at[len(copies)]))
        copies.append(pltpu.make_async_copy(h_dn.at[k], wide.at[i, 0], sem.at[len(copies)]))
    return copies


N_LOAD = 23


def link_values(ridx, table, lidx, weight, out):
    sub = lax.broadcasted_iota(jnp.int32, (8, LANES), 0)
    lane = lax.broadcasted_iota(jnp.int32, (8, LANES), 1)
    rows_per_turn = 4

    def turn(tt, carry):
        for q in range(rows_per_turn):
            t = tt * rows_per_turn + q
            lrow = jnp.broadcast_to(lidx[pl.ds(t, 1), :], (8, LANES))
            acc = jnp.zeros((8, LANES), jnp.float32)
            for g in range(LANES // 8):
                v = jnp.broadcast_to(table[pl.ds(ridx[t, 8 * g], 1), :], (8, LANES))
                for j in range(1, 8):
                    row = table[pl.ds(ridx[t, 8 * g + j], 1), :]
                    v = jnp.where(sub == j, jnp.broadcast_to(row, (8, LANES)), v)
                res = jnp.take_along_axis(v, lrow, axis=1)
                acc = jnp.where(lane // 8 == g, res, acc)
            acc = jnp.where(lane % 8 == sub, acc, 0.0)
            out[pl.ds(t, 1), :] = jnp.sum(acc, axis=0, keepdims=True) * weight[pl.ds(t, 1), :]
        return carry

    lax.fori_loop(0, OWNERS // rows_per_turn, turn, 0)


def step_kernel(
    ridx, lidx, weight, h_up, h_dn, v_up, v_dn, c7, c8, c9, c10, adj, saved, solid,
    out, values, wide, sav, sol, table, obuf, vup, vdn, load_sem, misc_sem, out_sem,
):
    copies = load_copies(adj, h_up, h_dn, wide, load_sem)
    for c in copies:
        c.start()
    misc = [
        pltpu.make_async_copy(saved, sav, misc_sem.at[0]),
        pltpu.make_async_copy(solid, sol, misc_sem.at[1]),
    ]
    for c in misc:
        c.start()
    for halo, rims, pops, corner in (
        (v_up, vup, VERT_UP, {7: c7, 10: c10}),
        (v_dn, vdn, VERT_DOWN, {8: c8, 9: c9}),
    ):
        for k, i in enumerate(pops):
            cs = VECS[i][0]
            for xt in range(COLS):
                span = slice(LANES * xt, LANES * (xt + 1))
                if cs == 0:
                    rims[k, xt] = halo[k, :, span]
                elif cs == 1:
                    rims[k, xt, 0 : CS - 1] = halo[k, 1:CS, span]
                    rims[k, xt, CS - 1 : CS] = corner[i][:, span]
                else:
                    rims[k, xt, 1:CS] = halo[k, 0 : CS - 1, span]
                    rims[k, xt, 0:1] = corner[i][:, span]
    for c in copies:
        c.wait()
    for c in misc:
        c.wait()

    vrow = lax.broadcasted_iota(jnp.int32, (CV, LANES), 0)
    lane = lax.broadcasted_iota(jnp.int32, (CV, LANES), 1)

    def slab(s, carry):
        rolled = {}

        def column(i, xt):
            cv = VECS[i][1]
            x = wide[i, s, :, LANES * xt : LANES * (xt + 1)]
            if cv == 1:
                rim = vup[VERT_UP.index(i), xt, pl.ds(s, 1), :]
                x = jnp.where(vrow == CV - 1, jnp.broadcast_to(rim, (CV, LANES)), pltpu.roll(x, CV - 1, 0))
            elif cv == -1:
                rim = vdn[VERT_DOWN.index(i), xt, pl.ds(s, 1), :]
                x = jnp.where(vrow == 0, jnp.broadcast_to(rim, (CV, LANES)), pltpu.roll(x, 1, 0))
            return x

        def rolled_column(i, xt):
            if (i, xt) not in rolled:
                rolled[i, xt] = pltpu.roll(column(i, xt), LANES - 1 if VECS[i][2] == 1 else 1, 1)
            return rolled[i, xt]

        for xt in range(COLS):
            pulled = []
            for i in range(Q):
                cx = VECS[i][2]
                if cx == 0:
                    pulled.append(column(i, xt))
                else:
                    here = rolled_column(i, xt)
                    beside = rolled_column(i, (xt + cx) % COLS)
                    edge = LANES - 1 if cx == 1 else 0
                    pulled.append(jnp.where(lane == edge, beside, here))
            sums = [pulled[2 * p + 1] + pulled[2 * p + 2] for p in range(PAIRS)]
            diffs = [pulled[2 * p + 1] - pulled[2 * p + 2] for p in range(PAIRS)]
            for p in range(PAIRS):
                for vt in range(2):
                    base = ((p * CS) * 2 + vt) * 64 + 8 * xt
                    table[pl.ds(pl.multiple_of(s * 128 + base, 8), 8), :] = diffs[p][8 * vt : 8 * vt + 8]

            def store(i, v):
                obuf[i, s, :, LANES * xt : LANES * (xt + 1)] = v

            collide(
                pulled, sums, diffs,
                lambda i: sav[i, s, :, LANES * xt : LANES * (xt + 1)].astype(jnp.float32),
                sol[s, :, LANES * xt : LANES * (xt + 1)] == 1,
                store,
            )
        pltpu.make_async_copy(obuf.at[:, s], out.at[:, s], out_sem.at[s]).start()
        return carry

    lax.fori_loop(0, CS, slab, 0)
    link_values(ridx, table, lidx, weight, values)
    for s in range(CS):
        pltpu.make_async_copy(obuf.at[:, s], out.at[:, s], out_sem.at[s]).wait()


def sums_kernel(slots, received, out):
    his = ELEM_DEV // LANES
    sub_lo = lax.broadcasted_iota(jnp.int32, (LANES, 2 * LANES), 0)
    sub_hi = lax.broadcasted_iota(jnp.int32, (his, 2 * LANES), 0)
    rows = OWNERS * CAP // (2 * LANES)

    def turn(t, acc):
        for q in range(4):
            r = t * 4 + q
            slot = slots[pl.ds(r, 1), :]
            v0 = received[pl.ds(r, 1), :]
            a = v0.astype(jnp.bfloat16).astype(jnp.float32)
            b = (v0 - a).astype(jnp.bfloat16).astype(jnp.float32)
            c = (v0 - a) - b
            hit = jnp.broadcast_to(slot >> 7, (his, 2 * LANES)) == sub_hi
            left = jnp.concatenate(
                [jnp.where(hit, jnp.broadcast_to(v, (his, 2 * LANES)), 0.0).astype(jnp.bfloat16) for v in (a, b, c)], 0
            )
            right = jnp.where(jnp.broadcast_to(slot & 127, (LANES, 2 * LANES)) == sub_lo, 1.0, 0.0).astype(jnp.bfloat16)
            acc = acc + lax.dot_general(
                left, right, (((1,), (1,)), ((), ())), preferred_element_type=jnp.float32
            )
        return acc

    acc = lax.fori_loop(0, rows // 4, turn, jnp.zeros((3 * his, LANES), jnp.float32))
    out[...] = acc[0:his] + acc[his : 2 * his] + acc[2 * his : 3 * his]


def halos(adjoint):
    ns = lax.axis_size("span")
    nv = lax.axis_size("vert")
    down = [(i, (i - 1) % ns) for i in range(ns)]
    up = [(i, (i + 1) % ns) for i in range(ns)]
    h_up = lax.ppermute(jnp.stack([adjoint[i, 0] for i in SPAN_UP], 0), "span", down)
    h_dn = lax.ppermute(jnp.stack([adjoint[i, CS - 1] for i in SPAN_DOWN], 0), "span", up)
    v_up = lax.ppermute(
        jnp.stack([adjoint[i, :, 0] for i in VERT_UP], 0), "vert", [(i, i - 1) for i in range(1, nv)]
    )
    v_dn = lax.ppermute(
        jnp.stack([adjoint[i, :, CV - 1] for i in VERT_DOWN], 0), "vert", [(i, i + 1) for i in range(nv - 1)]
    )
    corners = []
    for i in (7, 8, 9, 10):
        cs, cv, _ = VECS[i]
        pairs = []
        for a in range(ns):
            for b in range(nv):
                if 0 <= b + cv < nv:
                    pairs.append((((a + cs) % ns) * nv + b + cv, a * nv + b))
        piece = adjoint[i, 0 if cs == 1 else CS - 1, 0 if cv == 1 else CV - 1][None, :]
        corners.append(lax.ppermute(piece, ("span", "vert"), pairs))
    return h_up, h_dn, v_up, v_dn, corners


def body(adjoint, saved, solid, send_cells, send_dirs, send_weight, send_counts, recv_slots):
    h_up, h_dn, v_up, v_dn, corners = halos(adjoint)
    cells = send_cells[0]
    dirs = send_dirs[0]
    x_col = (cells >> 7) & 7
    v = (cells >> 10) & 15
    s = cells >> 14
    ridx = ((dirs - 1) >> 1) * 1024 + s * 128 + (v >> 3) * 64 + x_col * 8 + (v & 7)
    lidx = cells & 127
    live = jnp.arange(CAP, dtype=jnp.int32)[None, :] < send_counts[0][:, None]
    signed = jnp.where(dirs & 1 == 1, send_weight[0], -send_weight[0])
    weight = jnp.where(live, signed, 0.0)
    adjoint_prev, values = pl.pallas_call(
        step_kernel,
        out_shape=(
            jax.ShapeDtypeStruct((Q, CS, CV, NX), jnp.float32),
            jax.ShapeDtypeStruct((OWNERS, CAP), jnp.float32),
        ),
        in_specs=[SMEM, VMEM, VMEM, ANY, ANY, VMEM, VMEM, VMEM, VMEM, VMEM, VMEM, ANY, ANY, ANY],
        out_specs=(ANY, VMEM),
        scratch_shapes=[
            pltpu.VMEM((Q, CS, CV, NX), jnp.float32),
            pltpu.VMEM((Q, CS, CV, NX), jnp.bfloat16),
            pltpu.VMEM((CS, CV, NX), jnp.int32),
            pltpu.VMEM((ROWS, LANES), jnp.float32),
            pltpu.VMEM((Q, CS, CV, NX), jnp.float32),
            pltpu.VMEM((5, COLS, CS, LANES), jnp.float32),
            pltpu.VMEM((5, COLS, CS, LANES), jnp.float32),
            pltpu.SemaphoreType.DMA((N_LOAD,)),
            pltpu.SemaphoreType.DMA((2,)),
            pltpu.SemaphoreType.DMA((CS,)),
        ],
        compiler_params=pltpu.CompilerParams(vmem_limit_bytes=44 << 20),
        name="step",
    )(ridx, lidx, weight, h_up, h_dn, v_up, v_dn, *corners, adjoint, saved, solid)
    received = lax.all_to_all(values, ("span", "vert"), split_axis=0, concat_axis=0, tiled=True)
    sens = pl.pallas_call(
        sums_kernel,
        out_shape=jax.ShapeDtypeStruct((ELEM_DEV // LANES, LANES), jnp.float32),
        in_specs=[VMEM, VMEM],
        out_specs=VMEM,
        name="element_sums",
    )(recv_slots[0].reshape(64, 256), received.reshape(64, 256))
    return adjoint_prev, sens.reshape(ELEM_DEV)


def solution(mesh):
    return jax.shard_map(
        body,
        mesh=mesh,
        in_specs=(
            P(None, "span", "vert", None),
            P(None, "span", "vert", None),
            P("span", "vert", None),
            P(("span", "vert"), None, None),
            P(("span", "vert"), None, None),
            P(("span", "vert"), None, None),
            P(("span", "vert"), None),
            P(("span", "vert"), None, None),
        ),
        out_specs=(P(None, "span", "vert", None), P(("span", "vert"))),
        check_vma=False,
    )
```

```python
import jax
import jax.numpy as jnp
from jax import lax
from jax.experimental import pallas as pl
from jax.experimental.pallas import tpu as pltpu
from jax.sharding import PartitionSpec as P

Q = 19
CS = 8
CV = 16
NX = 1024
CAP = 128
OWNERS = 128
ELEM_DEV = 4096
PAIRS = 9
LANES = 128
COLS = NX // LANES
ROWS = PAIRS * CS * CV * COLS
OMEGA = 1.6

VECS = [
    (0, 0, 0),
    (1, 0, 0),
    (-1, 0, 0),
    (0, 1, 0),
    (0, -1, 0),
    (0, 0, 1),
    (0, 0, -1),
    (1, 1, 0),
    (-1, -1, 0),
    (1, -1, 0),
    (-1, 1, 0),
    (1, 0, 1),
    (-1, 0, -1),
    (1, 0, -1),
    (-1, 0, 1),
    (0, 1, 1),
    (0, -1, -1),
    (0, 1, -1),
    (0, -1, 1),
]
SPAN_UP = [i for i in range(Q) if VECS[i][0] == 1]
SPAN_DOWN = [i for i in range(Q) if VECS[i][0] == -1]
VERT_UP = [i for i in range(Q) if VECS[i][1] == 1]
VERT_DOWN = [i for i in range(Q) if VECS[i][1] == -1]

VMEM = pl.BlockSpec(memory_space=pltpu.VMEM)
SMEM = pl.BlockSpec(memory_space=pltpu.SMEM)
HBM = pl.BlockSpec(memory_space=pltpu.HBM)
SPAN_PAIRS = [p for p in range(PAIRS) if VECS[2 * p + 1][0] != 0]
SIDE_ROWS = 5 * CV * COLS
RIM_ROWS = 2 * SIDE_ROWS + 2 * 5 * CS * COLS
GROUPS = CAP // 8
LISTED = OWNERS * GROUPS
INNER = CS - 2


def collide(pulled, sums, diffs, saved, is_solid, store):
    f = [saved(i) for i in range(Q)]
    e = [None] * PAIRS
    o = [None] * PAIRS
    for p in range(PAIRS):
        e[p] = f[2 * p + 1] + f[2 * p + 2]
        o[p] = f[2 * p + 1] - f[2 * p + 2]
    rho = f[0] + ((e[0] + e[1]) + (e[2] + e[3])) + ((e[4] + e[5]) + (e[6] + e[7]) + e[8])
    us = (o[0] + ((o[3] + o[4]) + (o[5] + o[6]))) / rho
    uv = (o[1] + ((o[3] - o[4]) + (o[7] + o[8]))) / rho
    ux = (o[2] + ((o[5] - o[6]) + (o[7] - o[8]))) / rho
    usq = us * us + uv * uv + ux * ux
    d0, d1, d2, d3, d4, d5, d6, d7, d8 = diffs
    s0, s1, s2, s3, s4, s5, s6, s7, s8 = sums
    w = 1.0 / 36.0
    s34 = s3 + s4
    s56 = s5 + s6
    s78 = s7 + s8
    two0 = 2.0 * s0
    two1 = 2.0 * s1
    two2 = 2.0 * s2
    m0 = 12.0 * pulled[0] + (two0 + two1 + two2) + (s34 + s56 + s78)
    mss = two0 + s34 + s56
    mvv = two1 + s34 + s78
    mxx = two2 + s56 + s78
    msv = s3 - s4
    msx = s5 - s6
    mvx = s7 - s8
    ms = 2.0 * d0 + ((d3 + d4) + (d5 + d6))
    mv = 2.0 * d1 + ((d3 - d4) + (d7 + d8))
    mx = 2.0 * d2 + ((d5 - d6) + (d7 - d8))
    as_ = mss * us + msv * uv + msx * ux
    av = msv * us + mvv * uv + mvx * ux
    ax = msx * us + mvx * uv + mxx * ux
    k = OMEGA * w
    g = (k * m0) * (1.0 + 1.5 * usq) - (4.5 * k) * (us * as_ + uv * av + ux * ax)
    gs = (3.0 * k) * ((ms + 3.0 * as_) - us * m0)
    gv = (3.0 * k) * ((mv + 3.0 * av) - uv * m0)
    gx = (3.0 * k) * ((mx + 3.0 * ax) - ux * m0)
    keep = 1.0 - OMEGA
    store(0, jnp.where(is_solid, pulled[0], keep * pulled[0] + g))
    along = [gs, gv, gx, gs + gv, gs - gv, gs + gx, gs - gx, gv + gx, gv - gx]
    for p in range(PAIRS):
        a = pulled[2 * p + 1]
        b = pulled[2 * p + 2]
        store(2 * p + 1, jnp.where(is_solid, b, keep * a + (g + along[p])))
        store(2 * p + 2, jnp.where(is_solid, a, keep * b + (g - along[p])))


def col(xt):
    return slice(LANES * xt, LANES * (xt + 1))


def vert_shifted(x, rim, cv):
    if cv == 0:
        return x
    vrow = lax.broadcasted_iota(jnp.int32, (CV, LANES), 0)
    shifted = 0.0 if x is None else pltpu.roll(x, CV - 1 if cv == 1 else 1, 0)
    entering = 0.0 if rim is None else jnp.broadcast_to(rim, (CV, LANES))
    return jnp.where(vrow == (CV - 1 if cv == 1 else 0), entering, shifted)


def puller(column):
    lane = lax.broadcasted_iota(jnp.int32, (CV, LANES), 1)
    rolled = {}

    def rolled_column(i, xt):
        if (i, xt) not in rolled:
            rolled[i, xt] = pltpu.roll(column(i, xt), LANES - 1 if VECS[i][2] == 1 else 1, 1)
        return rolled[i, xt]

    def pulled(i, xt):
        cx = VECS[i][2]
        if cx == 0:
            return column(i, xt)
        here = rolled_column(i, xt)
        beside = rolled_column(i, (xt + cx) % COLS)
        return jnp.where(lane == (LANES - 1 if cx == 1 else 0), beside, here)

    return pulled


def ahead(x, dist):
    rows = x.shape[0]
    if dist >= LANES:
        return pltpu.roll(x, rows - dist // LANES, 0)
    lane = lax.broadcasted_iota(jnp.int32, x.shape, 1)
    here = pltpu.roll(x, LANES - dist, 1)
    return jnp.where(lane >= LANES - dist, pltpu.roll(here, rows - 1, 0), here)


def behind(x, dist):
    if dist >= LANES:
        return pltpu.roll(x, dist // LANES, 0)
    lane = lax.broadcasted_iota(jnp.int32, x.shape, 1)
    here = pltpu.roll(x, dist, 1)
    return jnp.where(lane < dist, pltpu.roll(here, 1, 0), here)


def compacted(flag, value, place, look_ahead, look_behind, size):
    count = flag
    dist = 1
    while dist < size:
        count = count + jnp.where(place >= dist, look_behind(count, dist), 0)
        dist *= 2
    item = jnp.where(flag == 1, ((place - (count - 1)) << 16) | (value << 1) | 1, 0)
    dist, bit = 1, 16
    while dist < size:
        other = look_ahead(item, dist)
        stays = jnp.where((item >> bit) & 1 == 0, item, 0)
        item = jnp.where((other >> bit) & 1 == 1, other, stays)
        dist *= 2
        bit += 1
    return (item & 0xFFFF) >> 1, count


def group_list(groups_row):
    shape = (GROUPS, LANES)
    sub = lax.broadcasted_iota(jnp.int32, shape, 0)
    lane = lax.broadcasted_iota(jnp.int32, shape, 1)
    mine = jnp.take_along_axis(jnp.broadcast_to(groups_row, shape), sub * 8 + (lane >> 4), axis=1)
    flag = jnp.where((lane & 15) < mine, 1, 0)
    place = sub * LANES + lane
    return compacted(flag, place, place, ahead, behind, LISTED)


def faces_kernel(adj, hv_up, hv_dn, tiles, sem):
    copies = []
    for k, i in enumerate(VERT_UP):
        copies.append(pltpu.make_async_copy(adj.at[i, :, pl.ds(0, 8)], tiles.at[k], sem.at[k]))
    for k, i in enumerate(VERT_DOWN):
        copies.append(pltpu.make_async_copy(adj.at[i, :, pl.ds(CV - 8, 8)], tiles.at[5 + k], sem.at[5 + k]))
    for c in copies:
        c.start()
    for k in range(10):
        copies[k].wait()
        for s in range(CS):
            if k < 5:
                hv_up[k, s : s + 1, :] = tiles[k, s, 0:1, :]
            else:
                hv_dn[k - 5, s : s + 1, :] = tiles[k, s, 7:8, :]


CHUNKS = 4
STEP = CS // CHUNKS
N_LOAD = 13


def load_copies(adj, wide, sem, q, lo, hi, first):
    copies = []
    for a, b in ((0, 1), (3, 7), (15, 19)):
        pops = pl.ds(a, b - a)
        copies.append((adj.at[pops, pl.ds(lo, hi - lo)], wide.at[pops, pl.ds(lo - first, hi - lo)]))
    for i in SPAN_UP:
        n = min(hi, CS - 1) - lo
        if n > 0:
            copies.append((adj.at[i, pl.ds(lo + 1, n)], wide.at[i, pl.ds(lo - first, n)]))
    for i in SPAN_DOWN:
        at = max(lo, 1)
        if hi > at:
            copies.append((adj.at[i, pl.ds(at - 1, hi - at)], wide.at[i, pl.ds(at - first, hi - at)]))
    return [pltpu.make_async_copy(a, b, sem.at[q, k]) for k, (a, b) in enumerate(copies)]


def tables_kernel(
    cells_ref, dirs_ref, weight_ref, counts_ref, adj,
    table, hs_up, hs_dn, ridx, hidx, lidx, pos, weight, list_a, list_b,
    wide, tilted, load_sem, face_sem,
):
    copies = [load_copies(adj, wide, load_sem, q, STEP * q, STEP * (q + 1), 0) for q in range(CHUNKS)]
    faces = []
    tilts = []
    for k in range(5):
        for i, s, out in ((SPAN_UP[k], 0, hs_up), (SPAN_DOWN[k], CS - 1, hs_dn)):
            dest = out.at[k]
            if VECS[i][1] != 0:
                tilts.append((len(tilts), VECS[i][1], out, k))
                dest = tilted.at[tilts[-1][0]]
            faces.append(pltpu.make_async_copy(adj.at[i, s], dest, face_sem.at[len(faces)]))
    for c in sum(copies, []) + faces:
        c.start()
    zero = jnp.zeros((CV, NX), jnp.float32)
    for i in SPAN_UP:
        wide[i, CS - 1] = zero
    for i in SPAN_DOWN:
        wide[i, 0] = zero

    cells = cells_ref[...]
    dirs = dirs_ref[...]
    pair = (dirs - 1) >> 1
    xc = (cells >> 7) & 7
    v = (cells >> 10) & 15
    s = cells >> 14
    in_slab = (v >> 3) * 64 + xc * 8 + (v & 7)
    ridx[...] = pair * 1024 + s * 128 + in_slab
    lidx[...] = cells & 127
    lane = lax.broadcasted_iota(jnp.int32, (OWNERS, CAP), 1)
    counts = jnp.broadcast_to(counts_ref[...].astype(jnp.float32), (OWNERS, OWNERS))
    live = lane.astype(jnp.float32) < jnp.transpose(counts)
    signed = jnp.where((dirs & 1) == 1, weight_ref[...], -weight_ref[...])
    weight[...] = jnp.where(live, signed, 0.0)
    has_s = (pair == 0) | ((pair >= 3) & (pair <= 6))
    k_s = jnp.where(pair == 0, 0, pair - 2)
    has_v = (pair == 1) | (pair == 3) | (pair == 4) | (pair >= 7)
    k_v = jnp.where(pair == 1, 0, jnp.where(pair < 7, pair - 2, pair - 4))
    on_s = has_s & ((s == 0) | (s == CS - 1))
    on_v = has_v & ((v == 0) | (v == CV - 1))
    at_s = (jnp.where(s == 0, 0, 5) + k_s) * 128 + in_slab
    at_v = 2 * SIDE_ROWS + ((jnp.where(v == 0, 0, 5) + k_v) * 8 + xc) * 8 + s
    flag = jnp.where(live & (on_s | on_v), 1, 0)
    where_rim = jnp.where(on_s, at_s, at_v)
    rows, count = compacted(
        flag, where_rim, lane,
        lambda x, d: pltpu.roll(x, CAP - d, 1), lambda x, d: pltpu.roll(x, d, 1), CAP,
    )
    hidx[...] = rows
    pos[...] = jnp.where(flag == 1, count - 1, -1)
    totals = jnp.transpose(count.astype(jnp.float32))[CAP - 1 : CAP, :].astype(jnp.int32)
    for out, groups in ((list_a, (counts_ref[...] + 7) >> 3), (list_b, (totals + 7) >> 3)):
        ids, running = group_list(groups)
        out[0:GROUPS, :] = ids
        out[GROUPS : 2 * GROUPS, :] = running
    list_b[2 * GROUPS : 2 * GROUPS + 8, :] = jnp.broadcast_to(jnp.max(totals, axis=1, keepdims=True), (8, LANES))
    list_a[2 * GROUPS : 2 * GROUPS + 8, :] = jnp.zeros((8, LANES), jnp.int32)

    def slab(s, carry):
        def column(i, xt):
            return vert_shifted(wide[i, s, :, col(xt)], None, VECS[i][1])

        pulled = puller(column)
        for xt in range(COLS):
            for p in range(PAIRS):
                diff = pulled(2 * p + 1, xt) - pulled(2 * p + 2, xt)
                for vt in range(2):
                    at = pl.multiple_of(s * 128 + (p * 1024 + 64 * vt + 8 * xt), 8)
                    table[pl.ds(at, 8), :] = diff[8 * vt : 8 * vt + 8]
        return carry

    for q in range(CHUNKS):
        for c in copies[q]:
            c.wait()
        lax.fori_loop(STEP * q, STEP * (q + 1), slab, 0)
    for c in faces:
        c.wait()
    for n, cv, out, k in tilts:
        for xt in range(COLS):
            out[k, :, col(xt)] = vert_shifted(tilted[n, :, col(xt)], None, cv)


PER_TURN = 32


def pick(group, index, table, lidx, picked):
    sub = lax.broadcasted_iota(jnp.int32, (8, LANES), 0)
    first = group * 8
    v = jnp.broadcast_to(table[pl.ds(index[first], 1), :], (8, LANES))
    for j in range(1, 8):
        row = table[pl.ds(index[first + j], 1), :]
        v = jnp.where(sub == j, jnp.broadcast_to(row, (8, LANES)), v)
    lrow = jnp.broadcast_to(lidx[pl.ds(group >> 4, 1), :], (8, LANES))
    picked[group] = jnp.take_along_axis(v, lrow, axis=1)


def pick_rest(start, listed, index, table, lidx, picked):
    total = listed[2 * LISTED - 1]

    def turn(m, carry):
        for q in range(PER_TURN):
            pick(listed[m * PER_TURN + q], index, table, lidx, picked)
        return carry

    lax.fori_loop(start // PER_TURN, (total + PER_TURN - 1) // PER_TURN, turn, 0)


def fill_rims(v_up, v_dn, vup, vdn):
    for halo, rims in ((v_up, vup), (v_dn, vdn)):
        for k in range(5):
            for xt in range(COLS):
                rims[k, xt] = halo[k, :, col(xt)]


def collide_column(pull, xt, sav, sol, obuf, s):
    pulled = [pull(i, xt) for i in range(Q)]
    sums = [pulled[2 * p + 1] + pulled[2 * p + 2] for p in range(PAIRS)]
    diffs = [pulled[2 * p + 1] - pulled[2 * p + 2] for p in range(PAIRS)]

    def store(i, v):
        obuf[i, s, :, col(xt)] = v

    collide(
        pulled, sums, diffs,
        lambda i: sav[i, s, :, col(xt)].astype(jnp.float32),
        sol[s, :, col(xt)] == 1,
        store,
    )


BESIDE = 24
IN_CHUNKS = 3
IN_STEP = INNER // IN_CHUNKS


def inner_kernel(
    index, listed, lidx, table, v_up, v_dn, adj, saved, solid,
    out, local, picked, wide, sav, sol, obuf, vup, vdn, load_sem, misc_sem, out_sem,
):
    copies = []
    for q in range(IN_CHUNKS):
        lo = 1 + IN_STEP * q
        copies.append(load_copies(adj, wide, load_sem, q, lo, lo + IN_STEP, 1))
        mine = pl.ds(IN_STEP * q, IN_STEP)
        copies[q].append(pltpu.make_async_copy(saved.at[:, pl.ds(lo, IN_STEP)], sav.at[:, mine], misc_sem.at[q, 0]))
        copies[q].append(pltpu.make_async_copy(solid.at[pl.ds(lo, IN_STEP)], sol.at[mine], misc_sem.at[q, 1]))
        for c in copies[q]:
            c.start()
    fill_rims(v_up, v_dn, vup, vdn)

    def slab(n, carry):
        def column(i, xt):
            cs, cv, _ = VECS[i]
            rim = None
            if cv != 0:
                src, own = (vup, VERT_UP) if cv == 1 else (vdn, VERT_DOWN)
                rim = src[own.index(i), xt, pl.ds(n + 1 + cs, 1), :]
            return vert_shifted(wide[i, n, :, col(xt)], rim, cv)

        pull = puller(column)
        for xt in range(COLS):
            collide_column(pull, xt, sav, sol, obuf, n)
            for q in range(BESIDE):
                pick(listed[(n * COLS + xt) * BESIDE + q], index, table, lidx, picked)
        pltpu.make_async_copy(obuf.at[:, n], out.at[:, n + 1], out_sem.at[n]).start()
        return carry

    for q in range(IN_CHUNKS):
        for c in copies[q]:
            c.wait()
        lax.fori_loop(IN_STEP * q, IN_STEP * (q + 1), slab, 0)
    pick_rest(INNER * COLS * BESIDE, listed, index, table, lidx, picked)
    sub = lax.broadcasted_iota(jnp.int32, (8, LANES), 0)
    lane = lax.broadcasted_iota(jnp.int32, (8, LANES), 1)

    def turn(b, carry):
        for q in range(8):
            t = b * 8 + q
            acc = picked[t * GROUPS]
            for g in range(1, GROUPS):
                acc = jnp.where((lane >> 3) == g, picked[t * GROUPS + g], acc)
            acc = jnp.where((lane & 7) == sub, acc, 0.0)
            local[pl.ds(t, 1), :] = jnp.sum(acc, axis=0, keepdims=True)
        return carry

    lax.fori_loop(0, OWNERS // 8, turn, 0)
    for n in range(INNER):
        pltpu.make_async_copy(obuf.at[:, n], out.at[:, n + 1], out_sem.at[n]).wait()


FIRST = 6


def rim_kernel(
    index, listed, lidx, pos, weight, local, h_up, h_dn, v_up, v_dn, values, rim, picked,
):
    for side, s, halo, pops in ((0, 0, h_dn, SPAN_DOWN), (1, CS - 1, h_up, SPAN_UP)):
        def column(i, xt):
            cs, cv, _ = VECS[i]
            if i in pops:
                return halo[pops.index(i), :, col(xt)]
            src, own = (v_up, VERT_UP) if cv == 1 else (v_dn, VERT_DOWN)
            return vert_shifted(None, src[own.index(i), s + cs : s + cs + 1, col(xt)], cv)

        pulled = puller(column)
        for k, p in enumerate(SPAN_PAIRS):
            plus, minus = 2 * p + 1, 2 * p + 2
            for xt in range(COLS):
                if VECS[plus][1] != 0:
                    d = pulled(plus, xt) - pulled(minus, xt)
                else:
                    d = pulled(plus, xt) if plus in pops else -pulled(minus, xt)
                for vt in range(2):
                    at = (side * 5 + k) * 128 + 64 * vt + 8 * xt
                    rim[at : at + 8, :] = d[8 * vt : 8 * vt + 8]
    lane = lax.broadcasted_iota(jnp.int32, (8, LANES), 1)
    sub = lax.broadcasted_iota(jnp.int32, (8, LANES), 0)
    for side, halo, pops in ((0, v_dn, VERT_DOWN), (1, v_up, VERT_UP)):
        for k, i in enumerate(pops):
            cs, _, cx = VECS[i]
            cols = [halo[k, :, col(xt)] for xt in range(COLS)]
            if cs != 0:
                cols = [pltpu.roll(c, CS - 1 if cs == 1 else 1, 0) for c in cols]
            if cx != 0:
                rolled = [pltpu.roll(c, LANES - 1 if cx == 1 else 1, 1) for c in cols]
                edge = LANES - 1 if cx == 1 else 0
                cols = [jnp.where(lane == edge, rolled[(xt + cx) % COLS], rolled[xt]) for xt in range(COLS)]
            for xt in range(COLS):
                at = 2 * SIDE_ROWS + ((side * 5 + k) * 8 + xt) * 8
                rim[at : at + 8, :] = cols[xt] if i % 2 == 1 else -cols[xt]

    pick_rest(0, listed, index, rim, lidx, picked)
    most = listed[2 * LISTED]

    def added(t, groups):
        posb = jnp.broadcast_to(pos[pl.ds(t, 1), :], (8, LANES))
        acc = jnp.zeros((8, LANES), jnp.float32)
        for g in groups:
            acc = acc + jnp.where(posb == sub + 8 * g, picked[t * GROUPS + g], 0.0)
        return jnp.sum(acc, axis=0, keepdims=True)

    def turn(b, carry):
        for q in range(8):
            t = b * 8 + q
            w = weight[pl.ds(t, 1), :]
            total = local[pl.ds(t, 1), :] + added(t, range(FIRST))
            values[pl.ds(t, 1), :] = jnp.where(w == 0.0, 0.0, w * total)
        return carry

    lax.fori_loop(0, OWNERS // 8, turn, 0)

    @pl.when(most > 8 * FIRST)
    def _():
        def more(t, carry):
            w = weight[pl.ds(t, 1), :]
            rest = w * added(t, range(FIRST, GROUPS))
            values[pl.ds(t, 1), :] = values[pl.ds(t, 1), :] + jnp.where(w == 0.0, 0.0, rest)
            return carry

        lax.fori_loop(0, OWNERS, more, 0)


def outer_kernel(
    h_up, h_dn, v_up, v_dn, adj, saved, solid, partial, out, wide, sav, sol, obuf, load_sem, out_sem,
):
    del partial
    ends = ((0, 0, h_dn, SPAN_DOWN), (1, CS - 1, h_up, SPAN_UP))
    copies = []
    for n, s, halo, pops in ends:
        moves = [
            (adj.at[pl.ds(a, b - a), s], wide.at[pl.ds(a, b - a), n]) for a, b in ((0, 1), (3, 7), (15, 19))
        ]
        for i in SPAN_UP + SPAN_DOWN:
            if i not in pops:
                moves.append((adj.at[i, s + VECS[i][0]], wide.at[i, n]))
        moves.append((saved.at[:, s], sav.at[:, n]))
        moves.append((solid.at[s], sol.at[n]))
        copies.append([pltpu.make_async_copy(a, b, load_sem.at[n, k]) for k, (a, b) in enumerate(moves)])
        for c in copies[n]:
            c.start()
    for n, s, halo, pops in ends:
        for c in copies[n]:
            c.wait()

        def column(i, xt):
            cs, cv, _ = VECS[i]
            if i in pops:
                return halo[pops.index(i), :, col(xt)]
            rim = None
            if cv != 0:
                src, own = (v_up, VERT_UP) if cv == 1 else (v_dn, VERT_DOWN)
                rim = src[own.index(i), s + cs : s + cs + 1, col(xt)]
            return vert_shifted(wide[i, n, :, col(xt)], rim, cv)

        pull = puller(column)
        for xt in range(COLS):
            collide_column(pull, xt, sav, sol, obuf, n)
        pltpu.make_async_copy(obuf.at[:, n], out.at[:, s], out_sem.at[n]).start()
    for n, s, halo, pops in ends:
        pltpu.make_async_copy(obuf.at[:, n], out.at[:, s], out_sem.at[n]).wait()


def sums_kernel(slots, received, out):
    his = ELEM_DEV // LANES
    sub_lo = lax.broadcasted_iota(jnp.int32, (LANES, 2 * LANES), 0)
    sub_hi = lax.broadcasted_iota(jnp.int32, (his, 2 * LANES), 0)

    def turn(t, acc):
        for q in range(8):
            r = (t * 8 + q) * 2
            slot = jnp.concatenate([slots[pl.ds(r, 1), :], slots[pl.ds(r + 1, 1), :]], 1)
            v0 = jnp.concatenate([received[r], received[r + 1]], 1)
            a = v0.astype(jnp.bfloat16).astype(jnp.float32)
            b = (v0 - a).astype(jnp.bfloat16).astype(jnp.float32)
            c = (v0 - a) - b
            hit = jnp.broadcast_to(slot >> 7, (his, 2 * LANES)) == sub_hi
            left = jnp.concatenate(
                [jnp.where(hit, jnp.broadcast_to(v, (his, 2 * LANES)), 0.0).astype(jnp.bfloat16) for v in (a, b, c)], 0
            )
            right = jnp.where(jnp.broadcast_to(slot & 127, (LANES, 2 * LANES)) == sub_lo, 1.0, 0.0).astype(jnp.bfloat16)
            acc = acc + lax.dot_general(
                left, right, (((1,), (1,)), ((), ())), preferred_element_type=jnp.float32
            )
        return acc

    acc = lax.fori_loop(0, OWNERS // 16, turn, jnp.zeros((3 * his, LANES), jnp.float32))
    out[...] = acc[0:his] + acc[his : 2 * his] + acc[2 * his : 3 * his]


def cost(us):
    return pl.CostEstimate(flops=0, bytes_accessed=int(us * 3.0e6), transcendentals=0)


def limit(mib):
    return pltpu.CompilerParams(vmem_limit_bytes=mib << 20)


F32 = jnp.float32
I32 = jnp.int32
GRID = (OWNERS, CAP)


def shape(dims, kind=F32):
    return jax.ShapeDtypeStruct(dims, kind)


def faces_call(adjoint):
    return pl.pallas_call(
        faces_kernel,
        out_shape=(shape((5, CS, NX)), shape((5, CS, NX))),
        in_specs=[HBM],
        out_specs=(VMEM, VMEM),
        scratch_shapes=[pltpu.VMEM((10, CS, 8, NX), F32), pltpu.SemaphoreType.DMA((10,))],
        compiler_params=limit(56),
        cost_estimate=cost(2),
        name="faces",
    )(adjoint)


def tables_call(cells, dirs, weight, counts, adjoint):
    return pl.pallas_call(
        tables_kernel,
        out_shape=(
            shape((ROWS, LANES)), shape((5, CV, NX)), shape((5, CV, NX)),
            shape(GRID, I32), shape(GRID, I32), shape(GRID, I32), shape(GRID, I32), shape(GRID),
            shape((40, LANES), I32), shape((40, LANES), I32),
        ),
        in_specs=[VMEM] * 4 + [HBM],
        out_specs=(VMEM,) * 10,
        scratch_shapes=[
            pltpu.VMEM((Q, CS, CV, NX), F32),
            pltpu.VMEM((4, CV, NX), F32),
            pltpu.SemaphoreType.DMA((CHUNKS, N_LOAD)),
            pltpu.SemaphoreType.DMA((10,)),
        ],
        compiler_params=limit(50),
        cost_estimate=cost(8),
        name="tables",
    )(cells, dirs, weight, counts, adjoint)


def inner_call(ridx, list_a, lidx, table, v_up, v_dn, adjoint, saved, solid):
    return pl.pallas_call(
        inner_kernel,
        out_shape=(shape((Q, CS, CV, NX)), shape(GRID)),
        in_specs=[SMEM, SMEM] + [VMEM] * 4 + [HBM] * 3,
        out_specs=(HBM, VMEM),
        scratch_shapes=[
            pltpu.VMEM((LISTED, 8, LANES), F32),
            pltpu.VMEM((Q, INNER, CV, NX), F32),
            pltpu.VMEM((Q, INNER, CV, NX), jnp.bfloat16),
            pltpu.VMEM((INNER, CV, NX), I32),
            pltpu.VMEM((Q, INNER, CV, NX), F32),
            pltpu.VMEM((5, COLS, CS, LANES), F32),
            pltpu.VMEM((5, COLS, CS, LANES), F32),
            pltpu.SemaphoreType.DMA((IN_CHUNKS, N_LOAD)),
            pltpu.SemaphoreType.DMA((IN_CHUNKS, 2)),
            pltpu.SemaphoreType.DMA((INNER,)),
        ],
        compiler_params=limit(50),
        cost_estimate=cost(15),
        name="inner",
    )(ridx.reshape(-1), list_a.reshape(-1), lidx, table, v_up, v_dn, adjoint, saved, solid)


def rim_call(hidx, list_b, lidx, pos, weight, local, h_up, h_dn, v_up, v_dn):
    return pl.pallas_call(
        rim_kernel,
        out_shape=shape(GRID),
        in_specs=[SMEM, SMEM] + [VMEM] * 8,
        out_specs=VMEM,
        scratch_shapes=[pltpu.VMEM((RIM_ROWS, LANES), F32), pltpu.VMEM((LISTED, 8, LANES), F32)],
        compiler_params=limit(50),
        cost_estimate=cost(5),
        name="rim",
    )(hidx.reshape(-1), list_b.reshape(-1), lidx, pos, weight, local, h_up, h_dn, v_up, v_dn)


def outer_call(h_up, h_dn, v_up, v_dn, adjoint, saved, solid, partial):
    return pl.pallas_call(
        outer_kernel,
        out_shape=shape((Q, CS, CV, NX)),
        in_specs=[VMEM] * 4 + [HBM] * 4,
        out_specs=HBM,
        scratch_shapes=[
            pltpu.VMEM((Q, 2, CV, NX), F32),
            pltpu.VMEM((Q, 2, CV, NX), jnp.bfloat16),
            pltpu.VMEM((2, CV, NX), I32),
            pltpu.VMEM((Q, 2, CV, NX), F32),
            pltpu.SemaphoreType.DMA((2, 10)),
            pltpu.SemaphoreType.DMA((2,)),
        ],
        input_output_aliases={7: 0},
        compiler_params=limit(56),
        cost_estimate=cost(3),
        name="outer",
    )(h_up, h_dn, v_up, v_dn, adjoint, saved, solid, partial)


def sums_call(slots, received):
    return pl.pallas_call(
        sums_kernel,
        out_shape=shape((ELEM_DEV // LANES, LANES)),
        in_specs=[VMEM, VMEM],
        out_specs=VMEM,
        cost_estimate=cost(4),
        name="element_sums",
    )(slots, received)


def body(adjoint, saved, solid, send_cells, send_dirs, send_weight, send_counts, recv_slots):
    ns = lax.axis_size("span")
    nv = lax.axis_size("vert")
    hv_up, hv_dn = faces_call(adjoint)
    v_up = lax.ppermute(hv_up, "vert", [(i, i - 1) for i in range(1, nv)])
    v_dn = lax.ppermute(hv_dn, "vert", [(i, i + 1) for i in range(nv - 1)])
    table, hs_up, hs_dn, ridx, hidx, lidx, pos, weight, list_a, list_b = tables_call(
        send_cells[0], send_dirs[0], send_weight[0], send_counts, adjoint
    )
    hs_up = hs_up.at[1, CV - 1].set(v_up[1, 0]).at[2, 0].set(v_dn[2, 0])
    hs_dn = hs_dn.at[1, 0].set(v_dn[1, CS - 1]).at[2, CV - 1].set(v_up[2, CS - 1])
    hs_up, hs_dn, list_a = lax.optimization_barrier((hs_up, hs_dn, list_a))
    h_up = lax.ppermute(hs_up, "span", [(i, (i - 1) % ns) for i in range(ns)])
    h_dn = lax.ppermute(hs_dn, "span", [(i, (i + 1) % ns) for i in range(ns)])
    partial, local = inner_call(ridx, list_a, lidx, table, v_up, v_dn, adjoint, saved, solid)
    values = rim_call(hidx, list_b, lidx, pos, weight, local, h_up, h_dn, v_up, v_dn)
    values, v_up, v_dn = lax.optimization_barrier((values, v_up, v_dn))
    received = lax.all_to_all(values[:, None, :], ("span", "vert"), split_axis=0, concat_axis=0, tiled=True)
    adjoint_prev = outer_call(h_up, h_dn, v_up, v_dn, adjoint, saved, solid, partial)
    sens = sums_call(recv_slots[0], received)
    return adjoint_prev, sens.reshape(ELEM_DEV)


def solution(mesh):
    return jax.shard_map(
        body,
        mesh=mesh,
        in_specs=(
            P(None, "span", "vert", None),
            P(None, "span", "vert", None),
            P("span", "vert", None),
            P(("span", "vert"), None, None),
            P(("span", "vert"), None, None),
            P(("span", "vert"), None, None),
            P(("span", "vert"), None),
            P(("span", "vert"), None, None),
        ),
        out_specs=(P(None, "span", "vert", None), P(("span", "vert"))),
        check_vma=False,
    )
```

```python
import jax
import jax.numpy as jnp
from jax import lax
from jax.experimental import pallas as pl
from jax.experimental.pallas import tpu as pltpu
from jax.sharding import PartitionSpec as P

Q = 19
CS = 8
CV = 16
NX = 1024
CAP = 128
OWNERS = 128
ELEM_DEV = 4096
PAIRS = 9
LANES = 128
COLS = NX // LANES
ROWS = PAIRS * CS * CV * COLS
OMEGA = 1.6

VECS = [
    (0, 0, 0),
    (1, 0, 0),
    (-1, 0, 0),
    (0, 1, 0),
    (0, -1, 0),
    (0, 0, 1),
    (0, 0, -1),
    (1, 1, 0),
    (-1, -1, 0),
    (1, -1, 0),
    (-1, 1, 0),
    (1, 0, 1),
    (-1, 0, -1),
    (1, 0, -1),
    (-1, 0, 1),
    (0, 1, 1),
    (0, -1, -1),
    (0, 1, -1),
    (0, -1, 1),
]
SPAN_UP = [i for i in range(Q) if VECS[i][0] == 1]
SPAN_DOWN = [i for i in range(Q) if VECS[i][0] == -1]
VERT_UP = [i for i in range(Q) if VECS[i][1] == 1]
VERT_DOWN = [i for i in range(Q) if VECS[i][1] == -1]

VMEM = pl.BlockSpec(memory_space=pltpu.VMEM)
SMEM = pl.BlockSpec(memory_space=pltpu.SMEM)
HBM = pl.BlockSpec(memory_space=pltpu.HBM)
SPAN_PAIRS = [p for p in range(PAIRS) if VECS[2 * p + 1][0] != 0]
VERT_PAIRS = [p for p in range(PAIRS) if VECS[2 * p + 1][1] != 0]
SIDE_ROWS = 5 * CV * COLS
RIM_ROWS = 2 * SIDE_ROWS + 2 * 5 * CS * COLS
GROUPS = CAP // 8
LISTED = OWNERS * GROUPS
INNER = CS - 2


def collide(pulled, sums, diffs, saved, is_solid, store):
    f = [saved(i) for i in range(Q)]
    e = [None] * PAIRS
    o = [None] * PAIRS
    for p in range(PAIRS):
        e[p] = f[2 * p + 1] + f[2 * p + 2]
        o[p] = f[2 * p + 1] - f[2 * p + 2]
    rho = f[0] + ((e[0] + e[1]) + (e[2] + e[3])) + ((e[4] + e[5]) + (e[6] + e[7]) + e[8])
    us = (o[0] + ((o[3] + o[4]) + (o[5] + o[6]))) / rho
    uv = (o[1] + ((o[3] - o[4]) + (o[7] + o[8]))) / rho
    ux = (o[2] + ((o[5] - o[6]) + (o[7] - o[8]))) / rho
    usq = us * us + uv * uv + ux * ux
    d0, d1, d2, d3, d4, d5, d6, d7, d8 = diffs
    s0, s1, s2, s3, s4, s5, s6, s7, s8 = sums
    w = 1.0 / 36.0
    s34 = s3 + s4
    s56 = s5 + s6
    s78 = s7 + s8
    two0 = 2.0 * s0
    two1 = 2.0 * s1
    two2 = 2.0 * s2
    m0 = 12.0 * pulled[0] + (two0 + two1 + two2) + (s34 + s56 + s78)
    mss = two0 + s34 + s56
    mvv = two1 + s34 + s78
    mxx = two2 + s56 + s78
    msv = s3 - s4
    msx = s5 - s6
    mvx = s7 - s8
    ms = 2.0 * d0 + ((d3 + d4) + (d5 + d6))
    mv = 2.0 * d1 + ((d3 - d4) + (d7 + d8))
    mx = 2.0 * d2 + ((d5 - d6) + (d7 - d8))
    as_ = mss * us + msv * uv + msx * ux
    av = msv * us + mvv * uv + mvx * ux
    ax = msx * us + mvx * uv + mxx * ux
    k = OMEGA * w
    g = (k * m0) * (1.0 + 1.5 * usq) - (4.5 * k) * (us * as_ + uv * av + ux * ax)
    gs = (3.0 * k) * ((ms + 3.0 * as_) - us * m0)
    gv = (3.0 * k) * ((mv + 3.0 * av) - uv * m0)
    gx = (3.0 * k) * ((mx + 3.0 * ax) - ux * m0)
    keep = 1.0 - OMEGA
    store(0, jnp.where(is_solid, pulled[0], keep * pulled[0] + g))
    along = [gs, gv, gx, gs + gv, gs - gv, gs + gx, gs - gx, gv + gx, gv - gx]
    for p in range(PAIRS):
        a = pulled[2 * p + 1]
        b = pulled[2 * p + 2]
        store(2 * p + 1, jnp.where(is_solid, b, keep * a + (g + along[p])))
        store(2 * p + 2, jnp.where(is_solid, a, keep * b + (g - along[p])))


def col(xt):
    return slice(LANES * xt, LANES * (xt + 1))


def vert_shifted(x, rim, cv):
    if cv == 0:
        return x
    vrow = lax.broadcasted_iota(jnp.int32, (CV, LANES), 0)
    shifted = 0.0 if x is None else pltpu.roll(x, CV - 1 if cv == 1 else 1, 0)
    entering = 0.0 if rim is None else jnp.broadcast_to(rim, (CV, LANES))
    return jnp.where(vrow == (CV - 1 if cv == 1 else 0), entering, shifted)


def puller(column):
    lane = lax.broadcasted_iota(jnp.int32, (CV, LANES), 1)
    rolled = {}

    def rolled_column(i, xt):
        if (i, xt) not in rolled:
            rolled[i, xt] = pltpu.roll(column(i, xt), LANES - 1 if VECS[i][2] == 1 else 1, 1)
        return rolled[i, xt]

    def pulled(i, xt):
        cx = VECS[i][2]
        if cx == 0:
            return column(i, xt)
        here = rolled_column(i, xt)
        beside = rolled_column(i, (xt + cx) % COLS)
        return jnp.where(lane == (LANES - 1 if cx == 1 else 0), beside, here)

    return pulled


def ahead(x, dist):
    rows = x.shape[0]
    if dist >= LANES:
        return pltpu.roll(x, rows - dist // LANES, 0)
    lane = lax.broadcasted_iota(jnp.int32, x.shape, 1)
    here = pltpu.roll(x, LANES - dist, 1)
    return jnp.where(lane >= LANES - dist, pltpu.roll(here, rows - 1, 0), here)


def behind(x, dist):
    if dist >= LANES:
        return pltpu.roll(x, dist // LANES, 0)
    lane = lax.broadcasted_iota(jnp.int32, x.shape, 1)
    here = pltpu.roll(x, dist, 1)
    return jnp.where(lane < dist, pltpu.roll(here, 1, 0), here)


def compacted(flag, value, place, look_ahead, look_behind, size):
    count = flag
    dist = 1
    while dist < size:
        count = count + jnp.where(place >= dist, look_behind(count, dist), 0)
        dist *= 2
    item = jnp.where(flag == 1, ((place - (count - 1)) << 16) | (value << 1) | 1, 0)
    dist, bit = 1, 16
    while dist < size:
        other = look_ahead(item, dist)
        stays = jnp.where((item >> bit) & 1 == 0, item, 0)
        item = jnp.where((other >> bit) & 1 == 1, other, stays)
        dist *= 2
        bit += 1
    return (item & 0xFFFF) >> 1, count


def group_list(groups_row):
    shape = (GROUPS, LANES)
    sub = lax.broadcasted_iota(jnp.int32, shape, 0)
    lane = lax.broadcasted_iota(jnp.int32, shape, 1)
    mine = jnp.take_along_axis(jnp.broadcast_to(groups_row, shape), sub * 8 + (lane >> 4), axis=1)
    flag = jnp.where((lane & 15) < mine, 1, 0)
    place = sub * LANES + lane
    return compacted(flag, place, place, ahead, behind, LISTED)


def row_lists(flag, value, rows, pos, listed):
    lane = lax.broadcasted_iota(jnp.int32, (OWNERS, CAP), 1)
    front, count = compacted(
        flag, value, lane,
        lambda x, d: pltpu.roll(x, CAP - d, 1), lambda x, d: pltpu.roll(x, d, 1), CAP,
    )
    rows[...] = front
    pos[...] = jnp.where(flag == 1, count - 1, -1)
    totals = jnp.transpose(count.astype(jnp.float32))[CAP - 1 : CAP, :].astype(jnp.int32)
    ids, running = group_list((totals + 7) >> 3)
    listed[0:GROUPS, :] = ids
    listed[GROUPS : 2 * GROUPS, :] = running
    listed[2 * GROUPS : 2 * GROUPS + 8, :] = jnp.broadcast_to(jnp.max(totals, axis=1, keepdims=True), (8, LANES))


def faces_kernel(adj, hv_up, hv_dn, tiles, sem):
    copies = []
    for k, i in enumerate(VERT_UP):
        copies.append(pltpu.make_async_copy(adj.at[i, :, pl.ds(0, 8)], tiles.at[k], sem.at[k]))
    for k, i in enumerate(VERT_DOWN):
        copies.append(pltpu.make_async_copy(adj.at[i, :, pl.ds(CV - 8, 8)], tiles.at[5 + k], sem.at[5 + k]))
    for c in copies:
        c.start()
    for k in range(10):
        copies[k].wait()
        for s in range(CS):
            if k < 5:
                hv_up[k, s : s + 1, :] = tiles[k, s, 0:1, :]
            else:
                hv_dn[k - 5, s : s + 1, :] = tiles[k, s, 7:8, :]


CHUNKS = 2
STEP = CS // CHUNKS
N_LOAD = 13


def load_copies(adj, wide, sem, q, lo, hi, first):
    copies = []
    for a, b in ((0, 1), (3, 7), (15, 19)):
        pops = pl.ds(a, b - a)
        copies.append((adj.at[pops, pl.ds(lo, hi - lo)], wide.at[pops, pl.ds(lo - first, hi - lo)]))
    for i in SPAN_UP:
        n = min(hi, CS - 1) - lo
        if n > 0:
            copies.append((adj.at[i, pl.ds(lo + 1, n)], wide.at[i, pl.ds(lo - first, n)]))
    for i in SPAN_DOWN:
        at = max(lo, 1)
        if hi > at:
            copies.append((adj.at[i, pl.ds(at - 1, hi - at)], wide.at[i, pl.ds(at - first, hi - at)]))
    return [pltpu.make_async_copy(a, b, sem.at[q, k]) for k, (a, b) in enumerate(copies)]


def tables_kernel(
    cells_ref, dirs_ref, weight_ref, counts_ref, adj,
    table, hs_up, hs_dn, ridx, lidx, pos, weight, list_a, rim_code,
    wide, tbuf, tilted, load_sem, face_sem, out_sem,
):
    copies = [load_copies(adj, wide, load_sem, q, STEP * q, STEP * (q + 1), 0) for q in range(CHUNKS)]
    faces = []
    tilts = []
    for k in range(5):
        for i, s, out in ((SPAN_UP[k], 0, hs_up), (SPAN_DOWN[k], CS - 1, hs_dn)):
            dest = out.at[k]
            if VECS[i][1] != 0:
                tilts.append((len(tilts), VECS[i][1], out, k))
                dest = tilted.at[tilts[-1][0]]
            faces.append(pltpu.make_async_copy(adj.at[i, s], dest, face_sem.at[len(faces)]))
    for c in sum(copies, []) + faces:
        c.start()
    zero = jnp.zeros((CV, NX), jnp.float32)
    for i in SPAN_UP:
        wide[i, CS - 1] = zero
    for i in SPAN_DOWN:
        wide[i, 0] = zero

    cells = cells_ref[...]
    dirs = dirs_ref[...]
    pair = (dirs - 1) >> 1
    xc = (cells >> 7) & 7
    v = (cells >> 10) & 15
    s = cells >> 14
    in_slab = (v >> 3) * 64 + xc * 8 + (v & 7)
    lidx[...] = cells & 127
    lane = lax.broadcasted_iota(jnp.int32, (OWNERS, CAP), 1)
    counts = jnp.broadcast_to(counts_ref[...].astype(jnp.float32), (OWNERS, OWNERS))
    live = lane.astype(jnp.float32) < jnp.transpose(counts)
    signed = jnp.where((dirs & 1) == 1, weight_ref[...], -weight_ref[...])
    weight[...] = jnp.where(live, signed, 0.0)
    has_s = (pair == 0) | ((pair >= 3) & (pair <= 6))
    k_s = jnp.where(pair == 0, 0, pair - 2)
    has_v = (pair == 1) | (pair == 3) | (pair == 4) | (pair >= 7)
    k_v = jnp.where(pair == 1, 0, jnp.where(pair < 7, pair - 2, pair - 4))
    on_s = has_s & ((s == 0) | (s == CS - 1))
    on_v = has_v & ((v == 0) | (v == CV - 1))
    at_s = (jnp.where(s == 0, 0, 5) + k_s) * 128 + in_slab
    at_v = 2 * SIDE_ROWS + ((jnp.where(v == 0, 0, 5) + k_v) * 8 + xc) * 8 + s
    on_rim = on_s | on_v
    rim_code[...] = jnp.where(live & on_rim, jnp.where(on_s, at_s, at_v), -1)
    flag = jnp.where(live & jnp.logical_not(on_rim), 1, 0)
    row_lists(flag, pair * 1024 + s * 128 + in_slab, ridx, pos, list_a)

    def slab(s, carry):
        def column(i, xt):
            return vert_shifted(wide[i, s, :, col(xt)], None, VECS[i][1])

        pulled = puller(column)
        for xt in range(COLS):
            for p in range(PAIRS):
                diff = pulled(2 * p + 1, xt) - pulled(2 * p + 2, xt)
                for vt in range(2):
                    at = pl.multiple_of(s * 128 + (64 * vt + 8 * xt), 8)
                    tbuf[p, pl.ds(at, 8), :] = diff[8 * vt : 8 * vt + 8]
        rows = pl.ds(pl.multiple_of(s * 128, 128), 128)
        pltpu.make_async_copy(tbuf.at[:, rows], table.at[:, rows], out_sem.at[s]).start()
        return carry

    for q in range(CHUNKS):
        for c in copies[q]:
            c.wait()
        lax.fori_loop(STEP * q, STEP * (q + 1), slab, 0)
    for c in faces:
        c.wait()
    for n, cv, out, k in tilts:
        for xt in range(COLS):
            out[k, :, col(xt)] = vert_shifted(tilted[n, :, col(xt)], None, cv)
    for s in range(CS):
        rows = pl.ds(s * 128, 128)
        pltpu.make_async_copy(tbuf.at[:, rows], table.at[:, rows], out_sem.at[s]).wait()


PER_TURN = 32


def pick(group, index, table, lidx, picked):
    sub = lax.broadcasted_iota(jnp.int32, (8, LANES), 0)
    first = group * 8
    v = jnp.broadcast_to(table[pl.ds(index[first], 1), :], (8, LANES))
    for j in range(1, 8):
        row = table[pl.ds(index[first + j], 1), :]
        v = jnp.where(sub == j, jnp.broadcast_to(row, (8, LANES)), v)
    lrow = jnp.broadcast_to(lidx[pl.ds(group >> 4, 1), :], (8, LANES))
    picked[group] = jnp.take_along_axis(v, lrow, axis=1)


def placed(t, groups, pos, picked):
    sub = lax.broadcasted_iota(jnp.int32, (8, LANES), 0)
    posb = jnp.broadcast_to(pos[pl.ds(t, 1), :], (8, LANES))
    acc = jnp.zeros((8, LANES), jnp.float32)
    for g in groups:
        acc = jnp.where(posb == sub + 8 * g, picked[t * GROUPS + g], acc)
    return jnp.sum(acc, axis=0, keepdims=True)


def pick_rest(start, listed, index, table, lidx, picked):
    total = listed[2 * LISTED - 1]

    def turn(m, carry):
        for q in range(PER_TURN):
            pick(listed[m * PER_TURN + q], index, table, lidx, picked)
        return carry

    lax.fori_loop(start // PER_TURN, (total + PER_TURN - 1) // PER_TURN, turn, 0)


def fill_rims(v_up, v_dn, vup, vdn):
    for halo, rims in ((v_up, vup), (v_dn, vdn)):
        for k in range(5):
            for xt in range(COLS):
                rims[k, xt] = halo[k, :, col(xt)]


def collide_column(pull, xt, sav, sol, obuf, s):
    pulled = [pull(i, xt) for i in range(Q)]
    sums = [pulled[2 * p + 1] + pulled[2 * p + 2] for p in range(PAIRS)]
    diffs = [pulled[2 * p + 1] - pulled[2 * p + 2] for p in range(PAIRS)]

    def store(i, v):
        obuf[i, s, :, col(xt)] = v

    collide(
        pulled, sums, diffs,
        lambda i: sav[i, s, :, col(xt)].astype(jnp.float32),
        sol[s, :, col(xt)] == 1,
        store,
    )


BESIDE = 27


def scalar_copies(index_ref, listed_ref, index, listed, sem):
    copies = [
        pltpu.make_async_copy(index_ref, index, sem.at[0]),
        pltpu.make_async_copy(listed_ref, listed, sem.at[1]),
    ]
    for c in copies:
        c.start()
    return copies


IN_CHUNKS = 3
IN_STEP = INNER // IN_CHUNKS


def inner_kernel(
    index_ref, listed_ref, lidx, pos, rim_code, v_up, v_dn, table_ref, adj, saved, solid,
    out, local, rim_index, rim_pos, rim_listed, near, index, listed, scalar_sem, table, table_sem, picked, wide, sav, sol, obuf, vup, vdn, load_sem, misc_sem, out_sem,
):
    scalars = scalar_copies(index_ref, listed_ref, index, listed, scalar_sem)
    scalars.append(pltpu.make_async_copy(table_ref, table, table_sem.at[0]))
    scalars[-1].start()
    copies = []
    for q in range(IN_CHUNKS):
        lo = 1 + IN_STEP * q
        copies.append(load_copies(adj, wide, load_sem, q, lo, lo + IN_STEP, 1))
        mine = pl.ds(IN_STEP * q, IN_STEP)
        copies[q].append(pltpu.make_async_copy(saved.at[:, pl.ds(lo, IN_STEP)], sav.at[:, mine], misc_sem.at[q, 0]))
        copies[q].append(pltpu.make_async_copy(solid.at[pl.ds(lo, IN_STEP)], sol.at[mine], misc_sem.at[q, 1]))
        for c in copies[q]:
            c.start()
    fill_rims(v_up, v_dn, vup, vdn)
    code = rim_code[...]
    row_lists(jnp.where(code >= 0, 1, 0), jnp.maximum(code, 0), rim_index, rim_pos, rim_listed)

    def slab(n, carry):
        def column(i, xt):
            cs, cv, _ = VECS[i]
            rim = None
            if cv != 0:
                src, own = (vup, VERT_UP) if cv == 1 else (vdn, VERT_DOWN)
                rim = src[own.index(i), xt, pl.ds(n + 1 + cs, 1), :]
            return vert_shifted(wide[i, n, :, col(xt)], rim, cv)

        pull = puller(column)
        for xt in range(COLS):
            collide_column(pull, xt, sav, sol, obuf, n)
            for q in range(BESIDE):
                pick(listed[(n * COLS + xt) * BESIDE + q], index, table, lidx, picked)
        pltpu.make_async_copy(obuf.at[:, n], out.at[:, n + 1], out_sem.at[n]).start()
        return carry

    for c in scalars:
        c.wait()
    for q in range(IN_CHUNKS):
        for c in copies[q]:
            c.wait()
        lax.fori_loop(IN_STEP * q, IN_STEP * (q + 1), slab, 0)
    pick_rest(INNER * COLS * BESIDE, listed, index, table, lidx, picked)

    def turn(b, carry):
        for q in range(16):
            t = b * 16 + q
            local[pl.ds(t, 1), :] = placed(t, range(GROUPS), pos, picked)
        return carry

    lax.fori_loop(0, OWNERS // 16, turn, 0)
    for side, s in ((0, 0), (1, CS - 1)):
        for k, p in enumerate(SPAN_PAIRS):
            at = (side * 5 + k) * 128
            own = p * 1024 + s * 128
            near[at : at + 128, :] = table[own : own + 128, :]
        for k, p in enumerate(VERT_PAIRS):
            for xt in range(COLS):
                at = 2 * SIDE_ROWS + ((side * 5 + k) * 8 + xt) * 8
                own = p * 1024 + (71 if side == 1 else 0) + 8 * xt
                near[at : at + 8, :] = table[pl.ds(own, CS, stride=128), :]
    for n in range(INNER):
        pltpu.make_async_copy(obuf.at[:, n], out.at[:, n + 1], out_sem.at[n]).wait()


FIRST = 6


def rim_kernel(
    index_ref, listed_ref, lidx, pos, weight, local, near, h_up, h_dn, v_up, v_dn, values,
    index, listed, scalar_sem, rim, picked,
):
    scalars = scalar_copies(index_ref, listed_ref, index, listed, scalar_sem)
    for side, s, halo, pops in ((0, 0, h_dn, SPAN_DOWN), (1, CS - 1, h_up, SPAN_UP)):
        def column(i, xt):
            cs, cv, _ = VECS[i]
            if i in pops:
                return halo[pops.index(i), :, col(xt)]
            src, own = (v_up, VERT_UP) if cv == 1 else (v_dn, VERT_DOWN)
            return vert_shifted(None, src[own.index(i), s + cs : s + cs + 1, col(xt)], cv)

        pulled = puller(column)
        for k, p in enumerate(SPAN_PAIRS):
            plus, minus = 2 * p + 1, 2 * p + 2
            for xt in range(COLS):
                if VECS[plus][1] != 0:
                    d = pulled(plus, xt) - pulled(minus, xt)
                else:
                    d = pulled(plus, xt) if plus in pops else -pulled(minus, xt)
                for vt in range(2):
                    at = (side * 5 + k) * 128 + 64 * vt + 8 * xt
                    rim[at : at + 8, :] = d[8 * vt : 8 * vt + 8] + near[at : at + 8, :]
    lane = lax.broadcasted_iota(jnp.int32, (8, LANES), 1)
    for side, halo, pops in ((0, v_dn, VERT_DOWN), (1, v_up, VERT_UP)):
        for k, i in enumerate(pops):
            cs, _, cx = VECS[i]
            cols = [halo[k, :, col(xt)] for xt in range(COLS)]
            if cs != 0:
                cols = [pltpu.roll(c, CS - 1 if cs == 1 else 1, 0) for c in cols]
            if cx != 0:
                rolled = [pltpu.roll(c, LANES - 1 if cx == 1 else 1, 1) for c in cols]
                edge = LANES - 1 if cx == 1 else 0
                cols = [jnp.where(lane == edge, rolled[(xt + cx) % COLS], rolled[xt]) for xt in range(COLS)]
            for xt in range(COLS):
                at = 2 * SIDE_ROWS + ((side * 5 + k) * 8 + xt) * 8
                here = near[at : at + 8, :]
                rim[at : at + 8, :] = here + cols[xt] if i % 2 == 1 else here - cols[xt]

    for c in scalars:
        c.wait()
    pick_rest(0, listed, index, rim, lidx, picked)
    most = listed[2 * LISTED]

    def turn(b, carry):
        for q in range(16):
            t = b * 16 + q
            w = weight[pl.ds(t, 1), :]
            total = local[pl.ds(t, 1), :] + placed(t, range(FIRST), pos, picked)
            values[pl.ds(t, 1), :] = jnp.where(w == 0.0, 0.0, w * total)
        return carry

    lax.fori_loop(0, OWNERS // 16, turn, 0)

    @pl.when(most > 8 * FIRST)
    def _():
        def more(t, carry):
            w = weight[pl.ds(t, 1), :]
            rest = w * placed(t, range(FIRST, GROUPS), pos, picked)
            values[pl.ds(t, 1), :] = values[pl.ds(t, 1), :] + jnp.where(w == 0.0, 0.0, rest)
            return carry

        lax.fori_loop(0, OWNERS, more, 0)


def outer_kernel(
    h_up, h_dn, v_up, v_dn, adj, saved, solid, recv, partial, out, slots, wide, sav, sol, obuf, load_sem, out_sem, slot_sem,
):
    del partial
    fetch = pltpu.make_async_copy(recv, slots, slot_sem.at[0])
    fetch.start()
    ends = ((0, 0, h_dn, SPAN_DOWN), (1, CS - 1, h_up, SPAN_UP))
    copies = []
    for n, s, halo, pops in ends:
        moves = [
            (adj.at[pl.ds(a, b - a), s], wide.at[pl.ds(a, b - a), n]) for a, b in ((0, 1), (3, 7), (15, 19))
        ]
        for i in SPAN_UP + SPAN_DOWN:
            if i not in pops:
                moves.append((adj.at[i, s + VECS[i][0]], wide.at[i, n]))
        moves.append((saved.at[:, s], sav.at[:, n]))
        moves.append((solid.at[s], sol.at[n]))
        copies.append([pltpu.make_async_copy(a, b, load_sem.at[n, k]) for k, (a, b) in enumerate(moves)])
        for c in copies[n]:
            c.start()
    for n, s, halo, pops in ends:
        for c in copies[n]:
            c.wait()

        def column(i, xt):
            cs, cv, _ = VECS[i]
            if i in pops:
                return halo[pops.index(i), :, col(xt)]
            rim = None
            if cv != 0:
                src, own = (v_up, VERT_UP) if cv == 1 else (v_dn, VERT_DOWN)
                rim = src[own.index(i), s + cs : s + cs + 1, col(xt)]
            return vert_shifted(wide[i, n, :, col(xt)], rim, cv)

        pull = puller(column)
        for xt in range(COLS):
            collide_column(pull, xt, sav, sol, obuf, n)
        pltpu.make_async_copy(obuf.at[:, n], out.at[:, s], out_sem.at[n]).start()
    for n, s, halo, pops in ends:
        pltpu.make_async_copy(obuf.at[:, n], out.at[:, s], out_sem.at[n]).wait()
    fetch.wait()


def sums_kernel(slots, received, out):
    his = ELEM_DEV // LANES
    sub_lo = lax.broadcasted_iota(jnp.int32, (LANES, 2 * LANES), 0)
    sub_hi = lax.broadcasted_iota(jnp.int32, (his, 2 * LANES), 0)

    acc = jnp.zeros((3 * his, LANES), jnp.float32)
    for r in range(0, OWNERS, 2):
        slot = jnp.concatenate([slots[r : r + 1, :], slots[r + 1 : r + 2, :]], 1)
        v0 = jnp.concatenate([received[r], received[r + 1]], 1)
        a = v0.astype(jnp.bfloat16).astype(jnp.float32)
        b = (v0 - a).astype(jnp.bfloat16).astype(jnp.float32)
        c = (v0 - a) - b
        hit = jnp.broadcast_to(slot >> 7, (his, 2 * LANES)) == sub_hi
        left = jnp.concatenate(
            [jnp.where(hit, jnp.broadcast_to(v, (his, 2 * LANES)), 0.0).astype(jnp.bfloat16) for v in (a, b, c)], 0
        )
        right = jnp.where(jnp.broadcast_to(slot & 127, (LANES, 2 * LANES)) == sub_lo, 1.0, 0.0).astype(jnp.bfloat16)
        acc = acc + lax.dot_general(left, right, (((1,), (1,)), ((), ())), preferred_element_type=jnp.float32)
    out[...] = acc[0:his] + acc[his : 2 * his] + acc[2 * his : 3 * his]


def cost(us):
    return pl.CostEstimate(flops=0, bytes_accessed=int(us * 3.0e6), transcendentals=0)


def limit(mib):
    return pltpu.CompilerParams(vmem_limit_bytes=mib << 20)


F32 = jnp.float32
I32 = jnp.int32
GRID = (OWNERS, CAP)


def shape(dims, kind=F32):
    return jax.ShapeDtypeStruct(dims, kind)


def faces_call(adjoint):
    return pl.pallas_call(
        faces_kernel,
        out_shape=(shape((5, CS, NX)), shape((5, CS, NX))),
        in_specs=[HBM],
        out_specs=(VMEM, VMEM),
        scratch_shapes=[pltpu.VMEM((10, CS, 8, NX), F32), pltpu.SemaphoreType.DMA((10,))],
        compiler_params=limit(56),
        cost_estimate=cost(2),
        name="faces",
    )(adjoint)


def tables_call(cells, dirs, weight, counts, adjoint):
    return pl.pallas_call(
        tables_kernel,
        out_shape=(
            shape((PAIRS, ROWS // PAIRS, LANES)), shape((5, CV, NX)), shape((5, CV, NX)),
            shape(GRID, I32), shape(GRID, I32), shape(GRID, I32), shape(GRID),
            shape((40, LANES), I32), shape(GRID, I32),
        ),
        in_specs=[VMEM] * 4 + [HBM],
        out_specs=(HBM,) + (VMEM,) * 8,
        scratch_shapes=[
            pltpu.VMEM((Q, CS, CV, NX), F32),
            pltpu.VMEM((PAIRS, ROWS // PAIRS, LANES), F32),
            pltpu.VMEM((4, CV, NX), F32),
            pltpu.SemaphoreType.DMA((CHUNKS, N_LOAD)),
            pltpu.SemaphoreType.DMA((10,)),
            pltpu.SemaphoreType.DMA((CS,)),
        ],
        compiler_params=limit(50),
        cost_estimate=cost(8),
        name="tables",
    )(cells, dirs, weight, counts, adjoint)


SCALARS = [pltpu.SMEM((OWNERS * CAP,), I32), pltpu.SMEM((40 * LANES,), I32), pltpu.SemaphoreType.DMA((2,))]


def inner_call(ridx, list_a, lidx, pos, rim_code, table, v_up, v_dn, adjoint, saved, solid):
    return pl.pallas_call(
        inner_kernel,
        out_shape=(
            shape((Q, CS, CV, NX)), shape(GRID), shape(GRID, I32), shape(GRID, I32), shape((40, LANES), I32),
            shape((RIM_ROWS, LANES)),
        ),
        in_specs=[VMEM] * 7 + [HBM] * 4,
        out_specs=(HBM,) + (VMEM,) * 5,
        scratch_shapes=SCALARS + [
            pltpu.VMEM((ROWS, LANES), F32),
            pltpu.SemaphoreType.DMA((1,)),
            pltpu.VMEM((LISTED, 8, LANES), F32),
            pltpu.VMEM((Q, INNER, CV, NX), F32),
            pltpu.VMEM((Q, INNER, CV, NX), jnp.bfloat16),
            pltpu.VMEM((INNER, CV, NX), I32),
            pltpu.VMEM((Q, INNER, CV, NX), F32),
            pltpu.VMEM((5, COLS, CS, LANES), F32),
            pltpu.VMEM((5, COLS, CS, LANES), F32),
            pltpu.SemaphoreType.DMA((IN_CHUNKS, N_LOAD)),
            pltpu.SemaphoreType.DMA((IN_CHUNKS, 2)),
            pltpu.SemaphoreType.DMA((INNER,)),
        ],
        compiler_params=limit(50),
        cost_estimate=cost(15),
        name="inner",
    )(ridx.reshape(-1), list_a.reshape(-1), lidx, pos, rim_code, v_up, v_dn, table.reshape(ROWS, LANES), adjoint, saved, solid)


def rim_call(hidx, list_b, lidx, pos, weight, local, near, h_up, h_dn, v_up, v_dn):
    return pl.pallas_call(
        rim_kernel,
        out_shape=shape(GRID),
        in_specs=[VMEM] * 11,
        out_specs=VMEM,
        scratch_shapes=SCALARS + [pltpu.VMEM((RIM_ROWS, LANES), F32), pltpu.VMEM((LISTED, 8, LANES), F32)],
        compiler_params=limit(50),
        cost_estimate=cost(5),
        name="rim",
    )(hidx.reshape(-1), list_b.reshape(-1), lidx, pos, weight, local, near, h_up, h_dn, v_up, v_dn)


OUTER_MIB = 53


def outer_call(h_up, h_dn, v_up, v_dn, adjoint, saved, solid, recv, partial):
    return pl.pallas_call(
        outer_kernel,
        out_shape=(shape((Q, CS, CV, NX)), shape(GRID, I32)),
        in_specs=[VMEM] * 4 + [HBM] * 5,
        out_specs=(HBM, VMEM),
        scratch_shapes=[
            pltpu.VMEM((Q, 2, CV, NX), F32),
            pltpu.VMEM((Q, 2, CV, NX), jnp.bfloat16),
            pltpu.VMEM((2, CV, NX), I32),
            pltpu.VMEM((Q, 2, CV, NX), F32),
            pltpu.SemaphoreType.DMA((2, 10)),
            pltpu.SemaphoreType.DMA((2,)),
            pltpu.SemaphoreType.DMA((1,)),
        ],
        input_output_aliases={8: 0},
        compiler_params=limit(OUTER_MIB),
        cost_estimate=cost(3),
        name="outer",
    )(h_up, h_dn, v_up, v_dn, adjoint, saved, solid, recv, partial)


def sums_call(slots, received):
    return pl.pallas_call(
        sums_kernel,
        out_shape=shape((ELEM_DEV // LANES, LANES)),
        in_specs=[VMEM, VMEM],
        out_specs=VMEM,
        compiler_params=limit(16),
        cost_estimate=cost(4),
        name="element_sums",
    )(slots, received)


def body(adjoint, saved, solid, send_cells, send_dirs, send_weight, send_counts, recv_slots):
    ns = lax.axis_size("span")
    nv = lax.axis_size("vert")
    hv_up, hv_dn = faces_call(adjoint)
    v_up = lax.ppermute(hv_up, "vert", [(i, i - 1) for i in range(1, nv)])
    v_dn = lax.ppermute(hv_dn, "vert", [(i, i + 1) for i in range(nv - 1)])
    table, hs_up, hs_dn, ridx, lidx, pos, weight, list_a, rim_code = tables_call(
        send_cells[0], send_dirs[0], send_weight[0], send_counts, adjoint
    )
    hs_up = hs_up.at[1, CV - 1].set(v_up[1, 0]).at[2, 0].set(v_dn[2, 0])
    hs_dn = hs_dn.at[1, 0].set(v_dn[1, CS - 1]).at[2, CV - 1].set(v_up[2, CS - 1])
    hs_up, hs_dn, list_a = lax.optimization_barrier((hs_up, hs_dn, list_a))
    h_up = lax.ppermute(hs_up, "span", [(i, (i - 1) % ns) for i in range(ns)])
    h_dn = lax.ppermute(hs_dn, "span", [(i, (i + 1) % ns) for i in range(ns)])
    partial, local, rim_index, rim_pos, list_b, near = inner_call(
        ridx, list_a, lidx, pos, rim_code, table, v_up, v_dn, adjoint, saved, solid
    )
    values = rim_call(rim_index, list_b, lidx, rim_pos, weight, local, near, h_up, h_dn, v_up, v_dn)
    values, v_up, v_dn = lax.optimization_barrier((values, v_up, v_dn))
    received = lax.all_to_all(values[:, None, :], ("span", "vert"), split_axis=0, concat_axis=0, tiled=True)
    adjoint_prev, slots = outer_call(h_up, h_dn, v_up, v_dn, adjoint, saved, solid, recv_slots[0], partial)
    sens = sums_call(slots, received)
    return adjoint_prev, sens.reshape(ELEM_DEV)


def solution(mesh):
    return jax.shard_map(
        body,
        mesh=mesh,
        in_specs=(
            P(None, "span", "vert", None),
            P(None, "span", "vert", None),
            P("span", "vert", None),
            P(("span", "vert"), None, None),
            P(("span", "vert"), None, None),
            P(("span", "vert"), None, None),
            P(("span", "vert"), None),
            P(("span", "vert"), None, None),
        ),
        out_specs=(P(None, "span", "vert", None), P(("span", "vert"))),
        check_vma=False,
    )
```

```python
import jax
import jax.numpy as jnp
from jax import lax
from jax.experimental import pallas as pl
from jax.experimental.pallas import tpu as pltpu
from jax.sharding import PartitionSpec as P

Q = 19
CS = 8
CV = 16
NX = 1024
CAP = 128
OWNERS = 128
ELEM_DEV = 4096
PAIRS = 9
LANES = 128
COLS = NX // LANES
ROWS = PAIRS * CS * CV * COLS
OMEGA = 1.6

VECS = [
    (0, 0, 0),
    (1, 0, 0),
    (-1, 0, 0),
    (0, 1, 0),
    (0, -1, 0),
    (0, 0, 1),
    (0, 0, -1),
    (1, 1, 0),
    (-1, -1, 0),
    (1, -1, 0),
    (-1, 1, 0),
    (1, 0, 1),
    (-1, 0, -1),
    (1, 0, -1),
    (-1, 0, 1),
    (0, 1, 1),
    (0, -1, -1),
    (0, 1, -1),
    (0, -1, 1),
]
SPAN_UP = [i for i in range(Q) if VECS[i][0] == 1]
SPAN_DOWN = [i for i in range(Q) if VECS[i][0] == -1]
VERT_UP = [i for i in range(Q) if VECS[i][1] == 1]
VERT_DOWN = [i for i in range(Q) if VECS[i][1] == -1]

VMEM = pl.BlockSpec(memory_space=pltpu.VMEM)
SMEM = pl.BlockSpec(memory_space=pltpu.SMEM)
HBM = pl.BlockSpec(memory_space=pltpu.HBM)
SPAN_PAIRS = [p for p in range(PAIRS) if VECS[2 * p + 1][0] != 0]
VERT_PAIRS = [p for p in range(PAIRS) if VECS[2 * p + 1][1] != 0]
SIDE_ROWS = 5 * CV * COLS
RIM_ROWS = 2 * SIDE_ROWS + 2 * 5 * CS * COLS
GROUPS = CAP // 8
LISTED = OWNERS * GROUPS
INNER = CS - 2


def collide(pulled, sums, diffs, saved, is_solid, store):
    f = [saved(i) for i in range(Q)]
    e = [None] * PAIRS
    o = [None] * PAIRS
    for p in range(PAIRS):
        e[p] = f[2 * p + 1] + f[2 * p + 2]
        o[p] = f[2 * p + 1] - f[2 * p + 2]
    rho = f[0] + ((e[0] + e[1]) + (e[2] + e[3])) + ((e[4] + e[5]) + (e[6] + e[7]) + e[8])
    us = (o[0] + ((o[3] + o[4]) + (o[5] + o[6]))) / rho
    uv = (o[1] + ((o[3] - o[4]) + (o[7] + o[8]))) / rho
    ux = (o[2] + ((o[5] - o[6]) + (o[7] - o[8]))) / rho
    usq = us * us + uv * uv + ux * ux
    d0, d1, d2, d3, d4, d5, d6, d7, d8 = diffs
    s0, s1, s2, s3, s4, s5, s6, s7, s8 = sums
    w = 1.0 / 36.0
    s34 = s3 + s4
    s56 = s5 + s6
    s78 = s7 + s8
    two0 = 2.0 * s0
    two1 = 2.0 * s1
    two2 = 2.0 * s2
    m0 = 12.0 * pulled[0] + (two0 + two1 + two2) + (s34 + s56 + s78)
    mss = two0 + s34 + s56
    mvv = two1 + s34 + s78
    mxx = two2 + s56 + s78
    msv = s3 - s4
    msx = s5 - s6
    mvx = s7 - s8
    ms = 2.0 * d0 + ((d3 + d4) + (d5 + d6))
    mv = 2.0 * d1 + ((d3 - d4) + (d7 + d8))
    mx = 2.0 * d2 + ((d5 - d6) + (d7 - d8))
    as_ = mss * us + msv * uv + msx * ux
    av = msv * us + mvv * uv + mvx * ux
    ax = msx * us + mvx * uv + mxx * ux
    k = OMEGA * w
    g = (k * m0) * (1.0 + 1.5 * usq) - (4.5 * k) * (us * as_ + uv * av + ux * ax)
    gs = (3.0 * k) * ((ms + 3.0 * as_) - us * m0)
    gv = (3.0 * k) * ((mv + 3.0 * av) - uv * m0)
    gx = (3.0 * k) * ((mx + 3.0 * ax) - ux * m0)
    keep = 1.0 - OMEGA
    store(0, jnp.where(is_solid, pulled[0], keep * pulled[0] + g))
    along = [gs, gv, gx, gs + gv, gs - gv, gs + gx, gs - gx, gv + gx, gv - gx]
    for p in range(PAIRS):
        a = pulled[2 * p + 1]
        b = pulled[2 * p + 2]
        store(2 * p + 1, jnp.where(is_solid, b, keep * a + (g + along[p])))
        store(2 * p + 2, jnp.where(is_solid, a, keep * b + (g - along[p])))


def col(xt):
    return slice(LANES * xt, LANES * (xt + 1))


def vert_shifted(x, rim, cv):
    if cv == 0:
        return x
    vrow = lax.broadcasted_iota(jnp.int32, (CV, LANES), 0)
    shifted = 0.0 if x is None else pltpu.roll(x, CV - 1 if cv == 1 else 1, 0)
    entering = 0.0 if rim is None else jnp.broadcast_to(rim, (CV, LANES))
    return jnp.where(vrow == (CV - 1 if cv == 1 else 0), entering, shifted)


def puller(column):
    lane = lax.broadcasted_iota(jnp.int32, (CV, LANES), 1)
    rolled = {}

    def rolled_column(i, xt):
        if (i, xt) not in rolled:
            rolled[i, xt] = pltpu.roll(column(i, xt), LANES - 1 if VECS[i][2] == 1 else 1, 1)
        return rolled[i, xt]

    def pulled(i, xt):
        cx = VECS[i][2]
        if cx == 0:
            return column(i, xt)
        here = rolled_column(i, xt)
        beside = rolled_column(i, (xt + cx) % COLS)
        return jnp.where(lane == (LANES - 1 if cx == 1 else 0), beside, here)

    return pulled


def ahead(x, dist):
    rows = x.shape[0]
    if dist >= LANES:
        return pltpu.roll(x, rows - dist // LANES, 0)
    lane = lax.broadcasted_iota(jnp.int32, x.shape, 1)
    here = pltpu.roll(x, LANES - dist, 1)
    return jnp.where(lane >= LANES - dist, pltpu.roll(here, rows - 1, 0), here)


def behind(x, dist):
    if dist >= LANES:
        return pltpu.roll(x, dist // LANES, 0)
    lane = lax.broadcasted_iota(jnp.int32, x.shape, 1)
    here = pltpu.roll(x, dist, 1)
    return jnp.where(lane < dist, pltpu.roll(here, 1, 0), here)


def compacted(flag, value, place, look_ahead, look_behind, size):
    count = flag
    dist = 1
    while dist < size:
        count = count + jnp.where(place >= dist, look_behind(count, dist), 0)
        dist *= 2
    item = jnp.where(flag == 1, ((place - (count - 1)) << 16) | (value << 1) | 1, 0)
    dist, bit = 1, 16
    while dist < size:
        other = look_ahead(item, dist)
        stays = jnp.where((item >> bit) & 1 == 0, item, 0)
        item = jnp.where((other >> bit) & 1 == 1, other, stays)
        dist *= 2
        bit += 1
    return (item & 0xFFFF) >> 1, count


def group_list(groups_row):
    shape = (GROUPS, LANES)
    sub = lax.broadcasted_iota(jnp.int32, shape, 0)
    lane = lax.broadcasted_iota(jnp.int32, shape, 1)
    mine = jnp.take_along_axis(jnp.broadcast_to(groups_row, shape), sub * 8 + (lane >> 4), axis=1)
    flag = jnp.where((lane & 15) < mine, 1, 0)
    place = sub * LANES + lane
    return compacted(flag, place, place, ahead, behind, LISTED)


def row_lists(flag, value, rows, pos, listed):
    lane = lax.broadcasted_iota(jnp.int32, (OWNERS, CAP), 1)
    front, count = compacted(
        flag, value, lane,
        lambda x, d: pltpu.roll(x, CAP - d, 1), lambda x, d: pltpu.roll(x, d, 1), CAP,
    )
    rows[...] = front
    pos[...] = jnp.where(flag == 1, count - 1, -1)
    totals = jnp.transpose(count.astype(jnp.float32))[CAP - 1 : CAP, :].astype(jnp.int32)
    ids, running = group_list((totals + 7) >> 3)
    listed[0:GROUPS, :] = ids
    listed[GROUPS : 2 * GROUPS, :] = running
    listed[2 * GROUPS : 2 * GROUPS + 8, :] = jnp.broadcast_to(jnp.max(totals, axis=1, keepdims=True), (8, LANES))


def faces_kernel(adj, hv_up, hv_dn, tiles, sem):
    copies = []
    for k, i in enumerate(VERT_UP):
        copies.append(pltpu.make_async_copy(adj.at[i, :, pl.ds(0, 8)], tiles.at[k], sem.at[k]))
    for k, i in enumerate(VERT_DOWN):
        copies.append(pltpu.make_async_copy(adj.at[i, :, pl.ds(CV - 8, 8)], tiles.at[5 + k], sem.at[5 + k]))
    for c in copies:
        c.start()
    for k in range(10):
        copies[k].wait()
        for s in range(CS):
            if k < 5:
                hv_up[k, s : s + 1, :] = tiles[k, s, 0:1, :]
            else:
                hv_dn[k - 5, s : s + 1, :] = tiles[k, s, 7:8, :]


CHUNKS = 2
STEP = CS // CHUNKS
N_LOAD = 13


def load_copies(adj, wide, sem, q, lo, hi, first):
    copies = []
    for a, b in ((0, 1), (3, 7), (15, 19)):
        pops = pl.ds(a, b - a)
        copies.append((adj.at[pops, pl.ds(lo, hi - lo)], wide.at[pops, pl.ds(lo - first, hi - lo)]))
    for i in SPAN_UP:
        n = min(hi, CS - 1) - lo
        if n > 0:
            copies.append((adj.at[i, pl.ds(lo + 1, n)], wide.at[i, pl.ds(lo - first, n)]))
    for i in SPAN_DOWN:
        at = max(lo, 1)
        if hi > at:
            copies.append((adj.at[i, pl.ds(at - 1, hi - at)], wide.at[i, pl.ds(at - first, hi - at)]))
    return [pltpu.make_async_copy(a, b, sem.at[q, k]) for k, (a, b) in enumerate(copies)]


def tables_kernel(
    cells_ref, dirs_ref, weight_ref, counts_ref, adj,
    table, hs_up, hs_dn, ridx, lidx, pos, weight, list_a, rim_code,
    wide, tbuf, tilted, load_sem, face_sem, out_sem,
):
    copies = [load_copies(adj, wide, load_sem, q, STEP * q, STEP * (q + 1), 0) for q in range(CHUNKS)]
    faces = []
    tilts = []
    for k in range(5):
        for i, s, out in ((SPAN_UP[k], 0, hs_up), (SPAN_DOWN[k], CS - 1, hs_dn)):
            dest = out.at[k]
            if VECS[i][1] != 0:
                tilts.append((len(tilts), VECS[i][1], out, k))
                dest = tilted.at[tilts[-1][0]]
            faces.append(pltpu.make_async_copy(adj.at[i, s], dest, face_sem.at[len(faces)]))
    for c in sum(copies, []) + faces:
        c.start()
    zero = jnp.zeros((CV, NX), jnp.float32)
    for i in SPAN_UP:
        wide[i, CS - 1] = zero
    for i in SPAN_DOWN:
        wide[i, 0] = zero

    cells = cells_ref[...]
    dirs = dirs_ref[...]
    pair = (dirs - 1) >> 1
    xc = (cells >> 7) & 7
    v = (cells >> 10) & 15
    s = cells >> 14
    in_slab = (v >> 3) * 64 + xc * 8 + (v & 7)
    lidx[...] = cells & 127
    lane = lax.broadcasted_iota(jnp.int32, (OWNERS, CAP), 1)
    counts = jnp.broadcast_to(counts_ref[...].astype(jnp.float32), (OWNERS, OWNERS))
    live = lane.astype(jnp.float32) < jnp.transpose(counts)
    signed = jnp.where((dirs & 1) == 1, weight_ref[...], -weight_ref[...])
    weight[...] = jnp.where(live, signed, 0.0)
    has_s = (pair == 0) | ((pair >= 3) & (pair <= 6))
    k_s = jnp.where(pair == 0, 0, pair - 2)
    has_v = (pair == 1) | (pair == 3) | (pair == 4) | (pair >= 7)
    k_v = jnp.where(pair == 1, 0, jnp.where(pair < 7, pair - 2, pair - 4))
    on_s = has_s & ((s == 0) | (s == CS - 1))
    on_v = has_v & ((v == 0) | (v == CV - 1))
    at_s = (jnp.where(s == 0, 0, 5) + k_s) * 128 + in_slab
    at_v = 2 * SIDE_ROWS + ((jnp.where(v == 0, 0, 5) + k_v) * 8 + xc) * 8 + s
    on_rim = on_s | on_v
    rim_code[...] = jnp.where(live & on_rim, jnp.where(on_s, at_s, at_v), -1)
    flag = jnp.where(live & jnp.logical_not(on_rim), 1, 0)
    row_lists(flag, pair * 1024 + s * 128 + in_slab, ridx, pos, list_a)

    def slab(s, carry):
        def column(i, xt):
            return vert_shifted(wide[i, s, :, col(xt)], None, VECS[i][1])

        pulled = puller(column)
        for xt in range(COLS):
            for p in range(PAIRS):
                diff = pulled(2 * p + 1, xt) - pulled(2 * p + 2, xt)
                for vt in range(2):
                    at = pl.multiple_of(s * 128 + (64 * vt + 8 * xt), 8)
                    tbuf[p, pl.ds(at, 8), :] = diff[8 * vt : 8 * vt + 8]
        rows = pl.ds(pl.multiple_of(s * 128, 128), 128)
        pltpu.make_async_copy(tbuf.at[:, rows], table.at[:, rows], out_sem.at[s]).start()
        return carry

    for q in range(CHUNKS):
        for c in copies[q]:
            c.wait()
        lax.fori_loop(STEP * q, STEP * (q + 1), slab, 0)
    for c in faces:
        c.wait()
    for n, cv, out, k in tilts:
        for xt in range(COLS):
            out[k, :, col(xt)] = vert_shifted(tilted[n, :, col(xt)], None, cv)
    for s in range(CS):
        rows = pl.ds(s * 128, 128)
        pltpu.make_async_copy(tbuf.at[:, rows], table.at[:, rows], out_sem.at[s]).wait()


PER_TURN = 32


def pick(group, index, table, lidx, picked):
    sub = lax.broadcasted_iota(jnp.int32, (8, LANES), 0)
    first = group * 8
    v = jnp.broadcast_to(table[pl.ds(index[first], 1), :], (8, LANES))
    for j in range(1, 8):
        row = table[pl.ds(index[first + j], 1), :]
        v = jnp.where(sub == j, jnp.broadcast_to(row, (8, LANES)), v)
    lrow = jnp.broadcast_to(lidx[pl.ds(group >> 4, 1), :], (8, LANES))
    picked[group] = jnp.take_along_axis(v, lrow, axis=1)


def placed(t, groups, pos, picked):
    sub = lax.broadcasted_iota(jnp.int32, (8, LANES), 0)
    posb = jnp.broadcast_to(pos[pl.ds(t, 1), :], (8, LANES))
    acc = jnp.zeros((8, LANES), jnp.float32)
    for g in groups:
        acc = jnp.where(posb == sub + 8 * g, picked[t * GROUPS + g], acc)
    return jnp.sum(acc, axis=0, keepdims=True)


def pick_some(first, last, listed, index, table, lidx, picked):
    def turn(m, carry):
        for q in range(PER_TURN):
            pick(listed[m * PER_TURN + q], index, table, lidx, picked)
        return carry

    lax.fori_loop(first, last, turn, 0)


def pick_rest(start, listed, index, table, lidx, picked):
    total = listed[2 * LISTED - 1]
    pick_some(start // PER_TURN, (total + PER_TURN - 1) // PER_TURN, listed, index, table, lidx, picked)


def fill_rims(v_up, v_dn, vup, vdn):
    for halo, rims in ((v_up, vup), (v_dn, vdn)):
        for k in range(5):
            for xt in range(COLS):
                rims[k, xt] = halo[k, :, col(xt)]


def collide_column(pull, xt, sav, sol, obuf, s):
    pulled = [pull(i, xt) for i in range(Q)]
    sums = [pulled[2 * p + 1] + pulled[2 * p + 2] for p in range(PAIRS)]
    diffs = [pulled[2 * p + 1] - pulled[2 * p + 2] for p in range(PAIRS)]

    def store(i, v):
        obuf[i, s, :, col(xt)] = v

    collide(
        pulled, sums, diffs,
        lambda i: sav[i, s, :, col(xt)].astype(jnp.float32),
        sol[s, :, col(xt)] == 1,
        store,
    )


AHEAD = 3 * PER_TURN
BESIDE = 25


def scalar_copies(index_ref, listed_ref, index, listed, sem):
    copies = [
        pltpu.make_async_copy(index_ref, index, sem.at[0]),
        pltpu.make_async_copy(listed_ref, listed, sem.at[1]),
    ]
    for c in copies:
        c.start()
    return copies


IN_CHUNKS = 3
IN_STEP = INNER // IN_CHUNKS


def inner_kernel(
    index_ref, listed_ref, lidx, pos, rim_code, v_up, v_dn, table_ref, adj, saved, solid,
    out, local, rim_index, rim_pos, rim_listed, near, index, listed, scalar_sem, table, table_sem, picked, wide, sav, sol, obuf, vup, vdn, load_sem, misc_sem, out_sem,
):
    scalars = scalar_copies(index_ref, listed_ref, index, listed, scalar_sem)
    scalars.append(pltpu.make_async_copy(table_ref, table, table_sem.at[0]))
    scalars[-1].start()
    copies = []
    for q in range(IN_CHUNKS):
        lo = 1 + IN_STEP * q
        copies.append(load_copies(adj, wide, load_sem, q, lo, lo + IN_STEP, 1))
        mine = pl.ds(IN_STEP * q, IN_STEP)
        copies[q].append(pltpu.make_async_copy(saved.at[:, pl.ds(lo, IN_STEP)], sav.at[:, mine], misc_sem.at[q, 0]))
        copies[q].append(pltpu.make_async_copy(solid.at[pl.ds(lo, IN_STEP)], sol.at[mine], misc_sem.at[q, 1]))
        for c in copies[q]:
            c.start()
    fill_rims(v_up, v_dn, vup, vdn)
    code = rim_code[...]
    row_lists(jnp.where(code >= 0, 1, 0), jnp.maximum(code, 0), rim_index, rim_pos, rim_listed)

    def slab(n, carry):
        def column(i, xt):
            cs, cv, _ = VECS[i]
            rim = None
            if cv != 0:
                src, own = (vup, VERT_UP) if cv == 1 else (vdn, VERT_DOWN)
                rim = src[own.index(i), xt, pl.ds(n + 1 + cs, 1), :]
            return vert_shifted(wide[i, n, :, col(xt)], rim, cv)

        pull = puller(column)
        for xt in range(COLS):
            collide_column(pull, xt, sav, sol, obuf, n)
            for q in range(BESIDE):
                pick(listed[AHEAD + (n * COLS + xt) * BESIDE + q], index, table, lidx, picked)
        pltpu.make_async_copy(obuf.at[:, n], out.at[:, n + 1], out_sem.at[n]).start()
        return carry

    for c in scalars:
        c.wait()
    for side, s in ((0, 0), (1, CS - 1)):
        for k, p in enumerate(SPAN_PAIRS):
            at = (side * 5 + k) * 128
            own = p * 1024 + s * 128
            near[at : at + 128, :] = table[own : own + 128, :]
        for k, p in enumerate(VERT_PAIRS):
            for xt in range(COLS):
                at = 2 * SIDE_ROWS + ((side * 5 + k) * 8 + xt) * 8
                own = p * 1024 + (71 if side == 1 else 0) + 8 * xt
                near[at : at + 8, :] = table[pl.ds(own, CS, stride=128), :]
    pick_some(0, AHEAD // PER_TURN, listed, index, table, lidx, picked)
    for q in range(IN_CHUNKS):
        for c in copies[q]:
            c.wait()
        lax.fori_loop(IN_STEP * q, IN_STEP * (q + 1), slab, 0)
    pick_rest(AHEAD + INNER * COLS * BESIDE, listed, index, table, lidx, picked)

    def turn(b, carry):
        for q in range(16):
            t = b * 16 + q
            local[pl.ds(t, 1), :] = placed(t, range(GROUPS), pos, picked)
        return carry

    lax.fori_loop(0, OWNERS // 16, turn, 0)
    for n in range(INNER):
        pltpu.make_async_copy(obuf.at[:, n], out.at[:, n + 1], out_sem.at[n]).wait()


FIRST = 6


def rim_kernel(
    index_ref, listed_ref, lidx, pos, weight, local, near, h_up, h_dn, v_up, v_dn, values,
    index, listed, scalar_sem, rim, picked,
):
    scalars = scalar_copies(index_ref, listed_ref, index, listed, scalar_sem)
    for side, s, halo, pops in ((0, 0, h_dn, SPAN_DOWN), (1, CS - 1, h_up, SPAN_UP)):
        def column(i, xt):
            cs, cv, _ = VECS[i]
            if i in pops:
                return halo[pops.index(i), :, col(xt)]
            src, own = (v_up, VERT_UP) if cv == 1 else (v_dn, VERT_DOWN)
            return vert_shifted(None, src[own.index(i), s + cs : s + cs + 1, col(xt)], cv)

        pulled = puller(column)
        for k, p in enumerate(SPAN_PAIRS):
            plus, minus = 2 * p + 1, 2 * p + 2
            for xt in range(COLS):
                if VECS[plus][1] != 0:
                    d = pulled(plus, xt) - pulled(minus, xt)
                else:
                    d = pulled(plus, xt) if plus in pops else -pulled(minus, xt)
                for vt in range(2):
                    at = (side * 5 + k) * 128 + 64 * vt + 8 * xt
                    rim[at : at + 8, :] = d[8 * vt : 8 * vt + 8] + near[at : at + 8, :]
    lane = lax.broadcasted_iota(jnp.int32, (8, LANES), 1)
    for side, halo, pops in ((0, v_dn, VERT_DOWN), (1, v_up, VERT_UP)):
        for k, i in enumerate(pops):
            cs, _, cx = VECS[i]
            cols = [halo[k, :, col(xt)] for xt in range(COLS)]
            if cs != 0:
                cols = [pltpu.roll(c, CS - 1 if cs == 1 else 1, 0) for c in cols]
            if cx != 0:
                rolled = [pltpu.roll(c, LANES - 1 if cx == 1 else 1, 1) for c in cols]
                edge = LANES - 1 if cx == 1 else 0
                cols = [jnp.where(lane == edge, rolled[(xt + cx) % COLS], rolled[xt]) for xt in range(COLS)]
            for xt in range(COLS):
                at = 2 * SIDE_ROWS + ((side * 5 + k) * 8 + xt) * 8
                here = near[at : at + 8, :]
                rim[at : at + 8, :] = here + cols[xt] if i % 2 == 1 else here - cols[xt]

    for c in scalars:
        c.wait()
    pick_rest(0, listed, index, rim, lidx, picked)
    most = listed[2 * LISTED]

    def turn(b, carry):
        for q in range(16):
            t = b * 16 + q
            w = weight[pl.ds(t, 1), :]
            total = local[pl.ds(t, 1), :] + placed(t, range(FIRST), pos, picked)
            values[pl.ds(t, 1), :] = jnp.where(w == 0.0, 0.0, w * total)
        return carry

    lax.fori_loop(0, OWNERS // 16, turn, 0)

    @pl.when(most > 8 * FIRST)
    def _():
        def more(t, carry):
            w = weight[pl.ds(t, 1), :]
            rest = w * placed(t, range(FIRST, GROUPS), pos, picked)
            values[pl.ds(t, 1), :] = values[pl.ds(t, 1), :] + jnp.where(w == 0.0, 0.0, rest)
            return carry

        lax.fori_loop(0, OWNERS, more, 0)


def outer_kernel(
    h_up, h_dn, v_up, v_dn, adj, saved, solid, recv, partial, out, slots, wide, sav, sol, obuf, load_sem, out_sem, slot_sem,
):
    del partial
    fetch = pltpu.make_async_copy(recv, slots, slot_sem.at[0])
    fetch.start()
    ends = ((0, 0, h_dn, SPAN_DOWN), (1, CS - 1, h_up, SPAN_UP))
    copies = []
    for n, s, halo, pops in ends:
        moves = [
            (adj.at[pl.ds(a, b - a), s], wide.at[pl.ds(a, b - a), n]) for a, b in ((0, 1), (3, 7), (15, 19))
        ]
        for i in SPAN_UP + SPAN_DOWN:
            if i not in pops:
                moves.append((adj.at[i, s + VECS[i][0]], wide.at[i, n]))
        moves.append((saved.at[:, s], sav.at[:, n]))
        moves.append((solid.at[s], sol.at[n]))
        copies.append([pltpu.make_async_copy(a, b, load_sem.at[n, k]) for k, (a, b) in enumerate(moves)])
        for c in copies[n]:
            c.start()
    for n, s, halo, pops in ends:
        for c in copies[n]:
            c.wait()

        def column(i, xt):
            cs, cv, _ = VECS[i]
            if i in pops:
                return halo[pops.index(i), :, col(xt)]
            rim = None
            if cv != 0:
                src, own = (v_up, VERT_UP) if cv == 1 else (v_dn, VERT_DOWN)
                rim = src[own.index(i), s + cs : s + cs + 1, col(xt)]
            return vert_shifted(wide[i, n, :, col(xt)], rim, cv)

        pull = puller(column)
        for xt in range(COLS):
            collide_column(pull, xt, sav, sol, obuf, n)
        pltpu.make_async_copy(obuf.at[:, n], out.at[:, s], out_sem.at[n]).start()
    for n, s, halo, pops in ends:
        pltpu.make_async_copy(obuf.at[:, n], out.at[:, s], out_sem.at[n]).wait()
    fetch.wait()


def sums_kernel(slots, received, out):
    his = ELEM_DEV // LANES
    sub_lo = lax.broadcasted_iota(jnp.int32, (LANES, 2 * LANES), 0)
    sub_hi = lax.broadcasted_iota(jnp.int32, (his, 2 * LANES), 0)

    acc = jnp.zeros((3 * his, LANES), jnp.float32)
    for r in range(0, OWNERS, 2):
        slot = jnp.concatenate([slots[r : r + 1, :], slots[r + 1 : r + 2, :]], 1)
        v0 = jnp.concatenate([received[r], received[r + 1]], 1)
        a = v0.astype(jnp.bfloat16).astype(jnp.float32)
        b = (v0 - a).astype(jnp.bfloat16).astype(jnp.float32)
        c = (v0 - a) - b
        hit = jnp.broadcast_to(slot >> 7, (his, 2 * LANES)) == sub_hi
        left = jnp.concatenate(
            [jnp.where(hit, jnp.broadcast_to(v, (his, 2 * LANES)), 0.0).astype(jnp.bfloat16) for v in (a, b, c)], 0
        )
        right = jnp.where(jnp.broadcast_to(slot & 127, (LANES, 2 * LANES)) == sub_lo, 1.0, 0.0).astype(jnp.bfloat16)
        acc = acc + lax.dot_general(left, right, (((1,), (1,)), ((), ())), preferred_element_type=jnp.float32)
    out[...] = acc[0:his] + acc[his : 2 * his] + acc[2 * his : 3 * his]


def cost(us):
    return pl.CostEstimate(flops=0, bytes_accessed=int(us * 3.0e6), transcendentals=0)


def limit(mib):
    return pltpu.CompilerParams(vmem_limit_bytes=mib << 20)


F32 = jnp.float32
I32 = jnp.int32
GRID = (OWNERS, CAP)


def shape(dims, kind=F32):
    return jax.ShapeDtypeStruct(dims, kind)


def faces_call(adjoint):
    return pl.pallas_call(
        faces_kernel,
        out_shape=(shape((5, CS, NX)), shape((5, CS, NX))),
        in_specs=[HBM],
        out_specs=(VMEM, VMEM),
        scratch_shapes=[pltpu.VMEM((10, CS, 8, NX), F32), pltpu.SemaphoreType.DMA((10,))],
        compiler_params=limit(56),
        cost_estimate=cost(2),
        name="faces",
    )(adjoint)


def tables_call(cells, dirs, weight, counts, adjoint):
    return pl.pallas_call(
        tables_kernel,
        out_shape=(
            shape((PAIRS, ROWS // PAIRS, LANES)), shape((5, CV, NX)), shape((5, CV, NX)),
            shape(GRID, I32), shape(GRID, I32), shape(GRID, I32), shape(GRID),
            shape((40, LANES), I32), shape(GRID, I32),
        ),
        in_specs=[VMEM] * 4 + [HBM],
        out_specs=(HBM,) + (VMEM,) * 8,
        scratch_shapes=[
            pltpu.VMEM((Q, CS, CV, NX), F32),
            pltpu.VMEM((PAIRS, ROWS // PAIRS, LANES), F32),
            pltpu.VMEM((4, CV, NX), F32),
            pltpu.SemaphoreType.DMA((CHUNKS, N_LOAD)),
            pltpu.SemaphoreType.DMA((10,)),
            pltpu.SemaphoreType.DMA((CS,)),
        ],
        compiler_params=limit(50),
        cost_estimate=cost(8),
        name="tables",
    )(cells, dirs, weight, counts, adjoint)


SCALARS = [pltpu.SMEM((OWNERS * CAP,), I32), pltpu.SMEM((40 * LANES,), I32), pltpu.SemaphoreType.DMA((2,))]


def inner_call(ridx, list_a, lidx, pos, rim_code, table, v_up, v_dn, adjoint, saved, solid):
    return pl.pallas_call(
        inner_kernel,
        out_shape=(
            shape((Q, CS, CV, NX)), shape(GRID), shape(GRID, I32), shape(GRID, I32), shape((40, LANES), I32),
            shape((RIM_ROWS, LANES)),
        ),
        in_specs=[VMEM] * 7 + [HBM] * 4,
        out_specs=(HBM,) + (VMEM,) * 5,
        scratch_shapes=SCALARS + [
            pltpu.VMEM((ROWS, LANES), F32),
            pltpu.SemaphoreType.DMA((1,)),
            pltpu.VMEM((LISTED, 8, LANES), F32),
            pltpu.VMEM((Q, INNER, CV, NX), F32),
            pltpu.VMEM((Q, INNER, CV, NX), jnp.bfloat16),
            pltpu.VMEM((INNER, CV, NX), I32),
            pltpu.VMEM((Q, INNER, CV, NX), F32),
            pltpu.VMEM((5, COLS, CS, LANES), F32),
            pltpu.VMEM((5, COLS, CS, LANES), F32),
            pltpu.SemaphoreType.DMA((IN_CHUNKS, N_LOAD)),
            pltpu.SemaphoreType.DMA((IN_CHUNKS, 2)),
            pltpu.SemaphoreType.DMA((INNER,)),
        ],
        compiler_params=limit(50),
        cost_estimate=cost(15),
        name="inner",
    )(ridx.reshape(-1), list_a.reshape(-1), lidx, pos, rim_code, v_up, v_dn, table.reshape(ROWS, LANES), adjoint, saved, solid)


def rim_call(hidx, list_b, lidx, pos, weight, local, near, h_up, h_dn, v_up, v_dn):
    return pl.pallas_call(
        rim_kernel,
        out_shape=shape(GRID),
        in_specs=[VMEM] * 11,
        out_specs=VMEM,
        scratch_shapes=SCALARS + [pltpu.VMEM((RIM_ROWS, LANES), F32), pltpu.VMEM((LISTED, 8, LANES), F32)],
        compiler_params=limit(50),
        cost_estimate=cost(5),
        name="rim",
    )(hidx.reshape(-1), list_b.reshape(-1), lidx, pos, weight, local, near, h_up, h_dn, v_up, v_dn)


OUTER_MIB = 53


def outer_call(h_up, h_dn, v_up, v_dn, adjoint, saved, solid, recv, partial):
    return pl.pallas_call(
        outer_kernel,
        out_shape=(shape((Q, CS, CV, NX)), shape(GRID, I32)),
        in_specs=[VMEM] * 4 + [HBM] * 5,
        out_specs=(HBM, VMEM),
        scratch_shapes=[
            pltpu.VMEM((Q, 2, CV, NX), F32),
            pltpu.VMEM((Q, 2, CV, NX), jnp.bfloat16),
            pltpu.VMEM((2, CV, NX), I32),
            pltpu.VMEM((Q, 2, CV, NX), F32),
            pltpu.SemaphoreType.DMA((2, 10)),
            pltpu.SemaphoreType.DMA((2,)),
            pltpu.SemaphoreType.DMA((1,)),
        ],
        input_output_aliases={8: 0},
        compiler_params=limit(OUTER_MIB),
        cost_estimate=cost(3),
        name="outer",
    )(h_up, h_dn, v_up, v_dn, adjoint, saved, solid, recv, partial)


def sums_call(slots, received):
    return pl.pallas_call(
        sums_kernel,
        out_shape=shape((ELEM_DEV // LANES, LANES)),
        in_specs=[VMEM, VMEM],
        out_specs=VMEM,
        compiler_params=limit(16),
        cost_estimate=cost(4),
        name="element_sums",
    )(slots, received)


def body(adjoint, saved, solid, send_cells, send_dirs, send_weight, send_counts, recv_slots):
    ns = lax.axis_size("span")
    nv = lax.axis_size("vert")
    hv_up, hv_dn = faces_call(adjoint)
    v_up = lax.ppermute(hv_up, "vert", [(i, i - 1) for i in range(1, nv)])
    v_dn = lax.ppermute(hv_dn, "vert", [(i, i + 1) for i in range(nv - 1)])
    table, hs_up, hs_dn, ridx, lidx, pos, weight, list_a, rim_code = tables_call(
        send_cells[0], send_dirs[0], send_weight[0], send_counts, adjoint
    )
    hs_up = hs_up.at[1, CV - 1].set(v_up[1, 0]).at[2, 0].set(v_dn[2, 0])
    hs_dn = hs_dn.at[1, 0].set(v_dn[1, CS - 1]).at[2, CV - 1].set(v_up[2, CS - 1])
    hs_up, hs_dn, list_a = lax.optimization_barrier((hs_up, hs_dn, list_a))
    h_up = lax.ppermute(hs_up, "span", [(i, (i - 1) % ns) for i in range(ns)])
    h_dn = lax.ppermute(hs_dn, "span", [(i, (i + 1) % ns) for i in range(ns)])
    partial, local, rim_index, rim_pos, list_b, near = inner_call(
        ridx, list_a, lidx, pos, rim_code, table, v_up, v_dn, adjoint, saved, solid
    )
    values = rim_call(rim_index, list_b, lidx, rim_pos, weight, local, near, h_up, h_dn, v_up, v_dn)
    values, v_up, v_dn = lax.optimization_barrier((values, v_up, v_dn))
    received = lax.all_to_all(values[:, None, :], ("span", "vert"), split_axis=0, concat_axis=0, tiled=True)
    adjoint_prev, slots = outer_call(h_up, h_dn, v_up, v_dn, adjoint, saved, solid, recv_slots[0], partial)
    sens = sums_call(slots, received)
    return adjoint_prev, sens.reshape(ELEM_DEV)


def solution(mesh):
    return jax.shard_map(
        body,
        mesh=mesh,
        in_specs=(
            P(None, "span", "vert", None),
            P(None, "span", "vert", None),
            P("span", "vert", None),
            P(("span", "vert"), None, None),
            P(("span", "vert"), None, None),
            P(("span", "vert"), None, None),
            P(("span", "vert"), None),
            P(("span", "vert"), None, None),
        ),
        out_specs=(P(None, "span", "vert", None), P(("span", "vert"))),
        check_vma=False,
    )
```

```python
import jax
import jax.numpy as jnp
from jax import lax
from jax.experimental import pallas as pl
from jax.experimental.pallas import tpu as pltpu
from jax.sharding import PartitionSpec as P

Q = 19
CS = 8
CV = 16
NX = 1024
CAP = 128
OWNERS = 128
ELEM_DEV = 4096
PAIRS = 9
LANES = 128
COLS = NX // LANES
ROWS = PAIRS * CS * CV * COLS
OMEGA = 1.6

VECS = [
    (0, 0, 0),
    (1, 0, 0),
    (-1, 0, 0),
    (0, 1, 0),
    (0, -1, 0),
    (0, 0, 1),
    (0, 0, -1),
    (1, 1, 0),
    (-1, -1, 0),
    (1, -1, 0),
    (-1, 1, 0),
    (1, 0, 1),
    (-1, 0, -1),
    (1, 0, -1),
    (-1, 0, 1),
    (0, 1, 1),
    (0, -1, -1),
    (0, 1, -1),
    (0, -1, 1),
]
SPAN_UP = [i for i in range(Q) if VECS[i][0] == 1]
SPAN_DOWN = [i for i in range(Q) if VECS[i][0] == -1]
VERT_UP = [i for i in range(Q) if VECS[i][1] == 1]
VERT_DOWN = [i for i in range(Q) if VECS[i][1] == -1]

VMEM = pl.BlockSpec(memory_space=pltpu.VMEM)
SMEM = pl.BlockSpec(memory_space=pltpu.SMEM)
HBM = pl.BlockSpec(memory_space=pltpu.HBM)
SPAN_PAIRS = [p for p in range(PAIRS) if VECS[2 * p + 1][0] != 0]
VERT_PAIRS = [p for p in range(PAIRS) if VECS[2 * p + 1][1] != 0]
SIDE_ROWS = 5 * CV * COLS
RIM_ROWS = 2 * SIDE_ROWS + 2 * 5 * CS * COLS
GROUPS = CAP // 8
LISTED = OWNERS * GROUPS
INNER = CS - 2


def collide(pulled, sums, diffs, saved, is_solid, store):
    f = [saved(i) for i in range(Q)]
    e = [None] * PAIRS
    o = [None] * PAIRS
    for p in range(PAIRS):
        e[p] = f[2 * p + 1] + f[2 * p + 2]
        o[p] = f[2 * p + 1] - f[2 * p + 2]
    rho = f[0] + ((e[0] + e[1]) + (e[2] + e[3])) + ((e[4] + e[5]) + (e[6] + e[7]) + e[8])
    us = (o[0] + ((o[3] + o[4]) + (o[5] + o[6]))) / rho
    uv = (o[1] + ((o[3] - o[4]) + (o[7] + o[8]))) / rho
    ux = (o[2] + ((o[5] - o[6]) + (o[7] - o[8]))) / rho
    usq = us * us + uv * uv + ux * ux
    d0, d1, d2, d3, d4, d5, d6, d7, d8 = diffs
    s0, s1, s2, s3, s4, s5, s6, s7, s8 = sums
    w = 1.0 / 36.0
    s34 = s3 + s4
    s56 = s5 + s6
    s78 = s7 + s8
    two0 = 2.0 * s0
    two1 = 2.0 * s1
    two2 = 2.0 * s2
    m0 = 12.0 * pulled[0] + (two0 + two1 + two2) + (s34 + s56 + s78)
    mss = two0 + s34 + s56
    mvv = two1 + s34 + s78
    mxx = two2 + s56 + s78
    msv = s3 - s4
    msx = s5 - s6
    mvx = s7 - s8
    ms = 2.0 * d0 + ((d3 + d4) + (d5 + d6))
    mv = 2.0 * d1 + ((d3 - d4) + (d7 + d8))
    mx = 2.0 * d2 + ((d5 - d6) + (d7 - d8))
    as_ = mss * us + msv * uv + msx * ux
    av = msv * us + mvv * uv + mvx * ux
    ax = msx * us + mvx * uv + mxx * ux
    k = OMEGA * w
    g = (k * m0) * (1.0 + 1.5 * usq) - (4.5 * k) * (us * as_ + uv * av + ux * ax)
    gs = (3.0 * k) * ((ms + 3.0 * as_) - us * m0)
    gv = (3.0 * k) * ((mv + 3.0 * av) - uv * m0)
    gx = (3.0 * k) * ((mx + 3.0 * ax) - ux * m0)
    keep = 1.0 - OMEGA
    store(0, jnp.where(is_solid, pulled[0], keep * pulled[0] + g))
    along = [gs, gv, gx, gs + gv, gs - gv, gs + gx, gs - gx, gv + gx, gv - gx]
    for p in range(PAIRS):
        a = pulled[2 * p + 1]
        b = pulled[2 * p + 2]
        store(2 * p + 1, jnp.where(is_solid, b, keep * a + (g + along[p])))
        store(2 * p + 2, jnp.where(is_solid, a, keep * b + (g - along[p])))


def col(xt):
    return slice(LANES * xt, LANES * (xt + 1))


def vert_shifted(x, rim, cv):
    if cv == 0:
        return x
    vrow = lax.broadcasted_iota(jnp.int32, (CV, LANES), 0)
    shifted = 0.0 if x is None else pltpu.roll(x, CV - 1 if cv == 1 else 1, 0)
    entering = 0.0 if rim is None else jnp.broadcast_to(rim, (CV, LANES))
    return jnp.where(vrow == (CV - 1 if cv == 1 else 0), entering, shifted)


def puller(column):
    lane = lax.broadcasted_iota(jnp.int32, (CV, LANES), 1)
    rolled = {}

    def rolled_column(i, xt):
        if (i, xt) not in rolled:
            rolled[i, xt] = pltpu.roll(column(i, xt), LANES - 1 if VECS[i][2] == 1 else 1, 1)
        return rolled[i, xt]

    def pulled(i, xt):
        cx = VECS[i][2]
        if cx == 0:
            return column(i, xt)
        here = rolled_column(i, xt)
        beside = rolled_column(i, (xt + cx) % COLS)
        return jnp.where(lane == (LANES - 1 if cx == 1 else 0), beside, here)

    return pulled


def ahead(x, dist):
    rows = x.shape[0]
    if dist >= LANES:
        return pltpu.roll(x, rows - dist // LANES, 0)
    lane = lax.broadcasted_iota(jnp.int32, x.shape, 1)
    here = pltpu.roll(x, LANES - dist, 1)
    return jnp.where(lane >= LANES - dist, pltpu.roll(here, rows - 1, 0), here)


def behind(x, dist):
    if dist >= LANES:
        return pltpu.roll(x, dist // LANES, 0)
    lane = lax.broadcasted_iota(jnp.int32, x.shape, 1)
    here = pltpu.roll(x, dist, 1)
    return jnp.where(lane < dist, pltpu.roll(here, 1, 0), here)


def compacted(flag, value, place, look_ahead, look_behind, size):
    count = flag
    dist = 1
    while dist < size:
        count = count + jnp.where(place >= dist, look_behind(count, dist), 0)
        dist *= 2
    item = jnp.where(flag == 1, ((place - (count - 1)) << 16) | (value << 1) | 1, 0)
    dist, bit = 1, 16
    while dist < size:
        other = look_ahead(item, dist)
        stays = jnp.where((item >> bit) & 1 == 0, item, 0)
        item = jnp.where((other >> bit) & 1 == 1, other, stays)
        dist *= 2
        bit += 1
    return (item & 0xFFFF) >> 1, count


def group_list(groups_row):
    shape = (GROUPS, LANES)
    sub = lax.broadcasted_iota(jnp.int32, shape, 0)
    lane = lax.broadcasted_iota(jnp.int32, shape, 1)
    mine = jnp.take_along_axis(jnp.broadcast_to(groups_row, shape), sub * 8 + (lane >> 4), axis=1)
    flag = jnp.where((lane & 15) < mine, 1, 0)
    place = sub * LANES + lane
    return compacted(flag, place, place, ahead, behind, LISTED)


def row_lists(flag, value, rows, pos, listed):
    lane = lax.broadcasted_iota(jnp.int32, (OWNERS, CAP), 1)
    front, count = compacted(
        flag, value, lane,
        lambda x, d: pltpu.roll(x, CAP - d, 1), lambda x, d: pltpu.roll(x, d, 1), CAP,
    )
    rows[...] = front
    pos[...] = jnp.where(flag == 1, count - 1, -1)
    totals = jnp.transpose(count.astype(jnp.float32))[CAP - 1 : CAP, :].astype(jnp.int32)
    ids, running = group_list((totals + 7) >> 3)
    listed[0:GROUPS, :] = ids
    listed[GROUPS : 2 * GROUPS, :] = running
    listed[2 * GROUPS : 2 * GROUPS + 8, :] = jnp.broadcast_to(jnp.max(totals, axis=1, keepdims=True), (8, LANES))


def faces_kernel(adj, hv_up, hv_dn, tiles, sem):
    copies = []
    for k, i in enumerate(VERT_UP):
        copies.append(pltpu.make_async_copy(adj.at[i, :, pl.ds(0, 8)], tiles.at[k], sem.at[k]))
    for k, i in enumerate(VERT_DOWN):
        copies.append(pltpu.make_async_copy(adj.at[i, :, pl.ds(CV - 8, 8)], tiles.at[5 + k], sem.at[5 + k]))
    for c in copies:
        c.start()
    for k in range(10):
        copies[k].wait()
        for s in range(CS):
            if k < 5:
                hv_up[k, s : s + 1, :] = tiles[k, s, 0:1, :]
            else:
                hv_dn[k - 5, s : s + 1, :] = tiles[k, s, 7:8, :]


CHUNKS = 2
STEP = CS // CHUNKS
N_LOAD = 13


def load_copies(adj, wide, sem, q, lo, hi, first):
    copies = []
    for a, b in ((0, 1), (3, 7), (15, 19)):
        pops = pl.ds(a, b - a)
        copies.append((adj.at[pops, pl.ds(lo, hi - lo)], wide.at[pops, pl.ds(lo - first, hi - lo)]))
    for i in SPAN_UP:
        n = min(hi, CS - 1) - lo
        if n > 0:
            copies.append((adj.at[i, pl.ds(lo + 1, n)], wide.at[i, pl.ds(lo - first, n)]))
    for i in SPAN_DOWN:
        at = max(lo, 1)
        if hi > at:
            copies.append((adj.at[i, pl.ds(at - 1, hi - at)], wide.at[i, pl.ds(at - first, hi - at)]))
    return [pltpu.make_async_copy(a, b, sem.at[q, k]) for k, (a, b) in enumerate(copies)]


def tables_kernel(
    cells_ref, dirs_ref, weight_ref, counts_ref, adj,
    table, hs_up, hs_dn, ridx, lidx, pos, weight, list_a, rim_code,
    wide, tbuf, tilted, load_sem, face_sem, out_sem,
):
    copies = [load_copies(adj, wide, load_sem, q, STEP * q, STEP * (q + 1), 0) for q in range(CHUNKS)]
    faces = []
    tilts = []
    for k in range(5):
        for i, s, out in ((SPAN_UP[k], 0, hs_up), (SPAN_DOWN[k], CS - 1, hs_dn)):
            dest = out.at[k]
            if VECS[i][1] != 0:
                tilts.append((len(tilts), VECS[i][1], out, k))
                dest = tilted.at[tilts[-1][0]]
            faces.append(pltpu.make_async_copy(adj.at[i, s], dest, face_sem.at[len(faces)]))
    for c in sum(copies, []) + faces:
        c.start()
    zero = jnp.zeros((CV, NX), jnp.float32)
    for i in SPAN_UP:
        wide[i, CS - 1] = zero
    for i in SPAN_DOWN:
        wide[i, 0] = zero

    cells = cells_ref[...]
    dirs = dirs_ref[...]
    pair = (dirs - 1) >> 1
    xc = (cells >> 7) & 7
    v = (cells >> 10) & 15
    s = cells >> 14
    in_slab = (v >> 3) * 64 + xc * 8 + (v & 7)
    lidx[...] = cells & 127
    lane = lax.broadcasted_iota(jnp.int32, (OWNERS, CAP), 1)
    counts = jnp.broadcast_to(counts_ref[...].astype(jnp.float32), (OWNERS, OWNERS))
    live = lane.astype(jnp.float32) < jnp.transpose(counts)
    signed = jnp.where((dirs & 1) == 1, weight_ref[...], -weight_ref[...])
    weight[...] = jnp.where(live, signed, 0.0)
    has_s = (pair == 0) | ((pair >= 3) & (pair <= 6))
    k_s = jnp.where(pair == 0, 0, pair - 2)
    has_v = (pair == 1) | (pair == 3) | (pair == 4) | (pair >= 7)
    k_v = jnp.where(pair == 1, 0, jnp.where(pair < 7, pair - 2, pair - 4))
    on_s = has_s & ((s == 0) | (s == CS - 1))
    on_v = has_v & ((v == 0) | (v == CV - 1))
    at_s = (jnp.where(s == 0, 0, 5) + k_s) * 128 + in_slab
    at_v = 2 * SIDE_ROWS + ((jnp.where(v == 0, 0, 5) + k_v) * 8 + xc) * 8 + s
    on_rim = on_s | on_v
    rim_code[...] = jnp.where(live & on_rim, jnp.where(on_s, at_s, at_v), -1)
    flag = jnp.where(live & jnp.logical_not(on_rim), 1, 0)
    row_lists(flag, pair * 1024 + s * 128 + in_slab, ridx, pos, list_a)

    def slab(s, carry):
        def column(i, xt):
            return vert_shifted(wide[i, s, :, col(xt)], None, VECS[i][1])

        pulled = puller(column)
        for xt in range(COLS):
            for p in range(PAIRS):
                diff = pulled(2 * p + 1, xt) - pulled(2 * p + 2, xt)
                for vt in range(2):
                    at = pl.multiple_of(s * 128 + (64 * vt + 8 * xt), 8)
                    tbuf[p, pl.ds(at, 8), :] = diff[8 * vt : 8 * vt + 8]
        rows = pl.ds(pl.multiple_of(s * 128, 128), 128)
        pltpu.make_async_copy(tbuf.at[:, rows], table.at[:, rows], out_sem.at[s]).start()
        return carry

    for q in range(CHUNKS):
        for c in copies[q]:
            c.wait()
        lax.fori_loop(STEP * q, STEP * (q + 1), slab, 0)
    for c in faces:
        c.wait()
    for n, cv, out, k in tilts:
        for xt in range(COLS):
            out[k, :, col(xt)] = vert_shifted(tilted[n, :, col(xt)], None, cv)
    for s in range(CS):
        rows = pl.ds(s * 128, 128)
        pltpu.make_async_copy(tbuf.at[:, rows], table.at[:, rows], out_sem.at[s]).wait()


PER_TURN = 32


def pick(group, index, table, lidx, picked):
    sub = lax.broadcasted_iota(jnp.int32, (8, LANES), 0)
    first = group * 8
    v = jnp.broadcast_to(table[pl.ds(index[first], 1), :], (8, LANES))
    for j in range(1, 8):
        row = table[pl.ds(index[first + j], 1), :]
        v = jnp.where(sub == j, jnp.broadcast_to(row, (8, LANES)), v)
    lrow = jnp.broadcast_to(lidx[pl.ds(group >> 4, 1), :], (8, LANES))
    picked[group] = jnp.take_along_axis(v, lrow, axis=1)


def placed(t, groups, pos, picked):
    sub = lax.broadcasted_iota(jnp.int32, (8, LANES), 0)
    posb = jnp.broadcast_to(pos[pl.ds(t, 1), :], (8, LANES))
    acc = jnp.zeros((8, LANES), jnp.float32)
    for g in groups:
        acc = jnp.where(posb == sub + 8 * g, picked[t * GROUPS + g], acc)
    return jnp.sum(acc, axis=0, keepdims=True)


def pick_some(first, last, listed, index, table, lidx, picked):
    def turn(m, carry):
        for q in range(PER_TURN):
            pick(listed[m * PER_TURN + q], index, table, lidx, picked)
        return carry

    lax.fori_loop(first, last, turn, 0)


def pick_rest(start, listed, index, table, lidx, picked):
    total = listed[2 * LISTED - 1]
    pick_some(start // PER_TURN, (total + PER_TURN - 1) // PER_TURN, listed, index, table, lidx, picked)


def fill_rims(v_up, v_dn, vup, vdn):
    for halo, rims in ((v_up, vup), (v_dn, vdn)):
        for k in range(5):
            for xt in range(COLS):
                rims[k, xt] = halo[k, :, col(xt)]


def collide_column(pull, xt, sav, sol, obuf, s, beside=None):
    pulled = [pull(i, xt) for i in range(Q)]
    sums = [pulled[2 * p + 1] + pulled[2 * p + 2] for p in range(PAIRS)]
    diffs = [pulled[2 * p + 1] - pulled[2 * p + 2] for p in range(PAIRS)]

    def store(i, v):
        obuf[i, s, :, col(xt)] = v
        if beside is not None:
            beside(i)

    collide(
        pulled, sums, diffs,
        lambda i: sav[i, s, :, col(xt)].astype(jnp.float32),
        sol[s, :, col(xt)] == 1,
        store,
    )


AHEAD = 3 * PER_TURN
BESIDE = 25


def scalar_copies(index_ref, listed_ref, index, listed, sem):
    copies = [
        pltpu.make_async_copy(index_ref, index, sem.at[0]),
        pltpu.make_async_copy(listed_ref, listed, sem.at[1]),
    ]
    for c in copies:
        c.start()
    return copies


IN_CHUNKS = 3
IN_STEP = INNER // IN_CHUNKS


def inner_kernel(
    index_ref, listed_ref, lidx, pos, rim_code, v_up, v_dn, table_ref, adj, saved, solid,
    out, local, rim_index, rim_pos, rim_listed, near, index, listed, scalar_sem, table, table_sem, picked, wide, sav, sol, obuf, vup, vdn, load_sem, misc_sem, out_sem,
):
    scalars = scalar_copies(index_ref, listed_ref, index, listed, scalar_sem)
    scalars.append(pltpu.make_async_copy(table_ref, table, table_sem.at[0]))
    scalars[-1].start()
    copies = []
    for q in range(IN_CHUNKS):
        lo = 1 + IN_STEP * q
        copies.append(load_copies(adj, wide, load_sem, q, lo, lo + IN_STEP, 1))
        mine = pl.ds(IN_STEP * q, IN_STEP)
        copies[q].append(pltpu.make_async_copy(saved.at[:, pl.ds(lo, IN_STEP)], sav.at[:, mine], misc_sem.at[q, 0]))
        copies[q].append(pltpu.make_async_copy(solid.at[pl.ds(lo, IN_STEP)], sol.at[mine], misc_sem.at[q, 1]))
        for c in copies[q]:
            c.start()
    fill_rims(v_up, v_dn, vup, vdn)
    code = rim_code[...]
    row_lists(jnp.where(code >= 0, 1, 0), jnp.maximum(code, 0), rim_index, rim_pos, rim_listed)

    def slab(n, carry):
        def column(i, xt):
            cs, cv, _ = VECS[i]
            rim = None
            if cv != 0:
                src, own = (vup, VERT_UP) if cv == 1 else (vdn, VERT_DOWN)
                rim = src[own.index(i), xt, pl.ds(n + 1 + cs, 1), :]
            return vert_shifted(wide[i, n, :, col(xt)], rim, cv)

        pull = puller(column)
        for xt in range(COLS):
            first = AHEAD + (n * COLS + xt) * BESIDE

            def beside(q):
                pick(listed[first + q], index, table, lidx, picked)

            for q in range(Q, BESIDE):
                beside(q)
            collide_column(pull, xt, sav, sol, obuf, n, beside)
        pltpu.make_async_copy(obuf.at[:, n], out.at[:, n + 1], out_sem.at[n]).start()
        return carry

    for c in scalars:
        c.wait()
    for side, s in ((0, 0), (1, CS - 1)):
        for k, p in enumerate(SPAN_PAIRS):
            at = (side * 5 + k) * 128
            own = p * 1024 + s * 128
            near[at : at + 128, :] = table[own : own + 128, :]
        for k, p in enumerate(VERT_PAIRS):
            for xt in range(COLS):
                at = 2 * SIDE_ROWS + ((side * 5 + k) * 8 + xt) * 8
                own = p * 1024 + (71 if side == 1 else 0) + 8 * xt
                near[at : at + 8, :] = table[pl.ds(own, CS, stride=128), :]
    pick_some(0, AHEAD // PER_TURN, listed, index, table, lidx, picked)
    for q in range(IN_CHUNKS):
        for c in copies[q]:
            c.wait()
        lax.fori_loop(IN_STEP * q, IN_STEP * (q + 1), slab, 0)
    pick_rest(AHEAD + INNER * COLS * BESIDE, listed, index, table, lidx, picked)

    def turn(b, carry):
        for q in range(16):
            t = b * 16 + q
            local[pl.ds(t, 1), :] = placed(t, range(GROUPS), pos, picked)
        return carry

    lax.fori_loop(0, OWNERS // 16, turn, 0)
    for n in range(INNER):
        pltpu.make_async_copy(obuf.at[:, n], out.at[:, n + 1], out_sem.at[n]).wait()


FIRST = 6


def rim_kernel(
    index_ref, listed_ref, lidx, pos, weight, local, near, h_up, h_dn, v_up, v_dn, values,
    index, listed, scalar_sem, rim, picked,
):
    scalars = scalar_copies(index_ref, listed_ref, index, listed, scalar_sem)
    for side, s, halo, pops in ((0, 0, h_dn, SPAN_DOWN), (1, CS - 1, h_up, SPAN_UP)):
        def column(i, xt):
            cs, cv, _ = VECS[i]
            if i in pops:
                return halo[pops.index(i), :, col(xt)]
            src, own = (v_up, VERT_UP) if cv == 1 else (v_dn, VERT_DOWN)
            return vert_shifted(None, src[own.index(i), s + cs : s + cs + 1, col(xt)], cv)

        pulled = puller(column)
        for k, p in enumerate(SPAN_PAIRS):
            plus, minus = 2 * p + 1, 2 * p + 2
            for xt in range(COLS):
                if VECS[plus][1] != 0:
                    d = pulled(plus, xt) - pulled(minus, xt)
                else:
                    d = pulled(plus, xt) if plus in pops else -pulled(minus, xt)
                for vt in range(2):
                    at = (side * 5 + k) * 128 + 64 * vt + 8 * xt
                    rim[at : at + 8, :] = d[8 * vt : 8 * vt + 8] + near[at : at + 8, :]
    lane = lax.broadcasted_iota(jnp.int32, (8, LANES), 1)
    for side, halo, pops in ((0, v_dn, VERT_DOWN), (1, v_up, VERT_UP)):
        for k, i in enumerate(pops):
            cs, _, cx = VECS[i]
            cols = [halo[k, :, col(xt)] for xt in range(COLS)]
            if cs != 0:
                cols = [pltpu.roll(c, CS - 1 if cs == 1 else 1, 0) for c in cols]
            if cx != 0:
                rolled = [pltpu.roll(c, LANES - 1 if cx == 1 else 1, 1) for c in cols]
                edge = LANES - 1 if cx == 1 else 0
                cols = [jnp.where(lane == edge, rolled[(xt + cx) % COLS], rolled[xt]) for xt in range(COLS)]
            for xt in range(COLS):
                at = 2 * SIDE_ROWS + ((side * 5 + k) * 8 + xt) * 8
                here = near[at : at + 8, :]
                rim[at : at + 8, :] = here + cols[xt] if i % 2 == 1 else here - cols[xt]

    for c in scalars:
        c.wait()
    pick_rest(0, listed, index, rim, lidx, picked)
    most = listed[2 * LISTED]

    def turn(b, carry):
        for q in range(16):
            t = b * 16 + q
            w = weight[pl.ds(t, 1), :]
            total = local[pl.ds(t, 1), :] + placed(t, range(FIRST), pos, picked)
            values[pl.ds(t, 1), :] = jnp.where(w == 0.0, 0.0, w * total)
        return carry

    lax.fori_loop(0, OWNERS // 16, turn, 0)

    @pl.when(most > 8 * FIRST)
    def _():
        def more(t, carry):
            w = weight[pl.ds(t, 1), :]
            rest = w * placed(t, range(FIRST, GROUPS), pos, picked)
            values[pl.ds(t, 1), :] = values[pl.ds(t, 1), :] + jnp.where(w == 0.0, 0.0, rest)
            return carry

        lax.fori_loop(0, OWNERS, more, 0)


def outer_kernel(
    h_up, h_dn, v_up, v_dn, adj, saved, solid, recv, partial, out, slots, wide, sav, sol, obuf, load_sem, out_sem, slot_sem,
):
    del partial
    fetch = pltpu.make_async_copy(recv, slots, slot_sem.at[0])
    fetch.start()
    ends = ((0, 0, h_dn, SPAN_DOWN), (1, CS - 1, h_up, SPAN_UP))
    copies = []
    for n, s, halo, pops in ends:
        moves = [
            (adj.at[pl.ds(a, b - a), s], wide.at[pl.ds(a, b - a), n]) for a, b in ((0, 1), (3, 7), (15, 19))
        ]
        for i in SPAN_UP + SPAN_DOWN:
            if i not in pops:
                moves.append((adj.at[i, s + VECS[i][0]], wide.at[i, n]))
        moves.append((saved.at[:, s], sav.at[:, n]))
        moves.append((solid.at[s], sol.at[n]))
        copies.append([pltpu.make_async_copy(a, b, load_sem.at[n, k]) for k, (a, b) in enumerate(moves)])
        for c in copies[n]:
            c.start()
    for n, s, halo, pops in ends:
        for c in copies[n]:
            c.wait()

        def column(i, xt):
            cs, cv, _ = VECS[i]
            if i in pops:
                return halo[pops.index(i), :, col(xt)]
            rim = None
            if cv != 0:
                src, own = (v_up, VERT_UP) if cv == 1 else (v_dn, VERT_DOWN)
                rim = src[own.index(i), s + cs : s + cs + 1, col(xt)]
            return vert_shifted(wide[i, n, :, col(xt)], rim, cv)

        pull = puller(column)
        for xt in range(COLS):
            collide_column(pull, xt, sav, sol, obuf, n)
        pltpu.make_async_copy(obuf.at[:, n], out.at[:, s], out_sem.at[n]).start()
    for n, s, halo, pops in ends:
        pltpu.make_async_copy(obuf.at[:, n], out.at[:, s], out_sem.at[n]).wait()
    fetch.wait()


def sums_kernel(slots, received, out):
    his = ELEM_DEV // LANES
    sub_lo = lax.broadcasted_iota(jnp.int32, (LANES, 2 * LANES), 0)
    sub_hi = lax.broadcasted_iota(jnp.int32, (his, 2 * LANES), 0)

    acc = jnp.zeros((3 * his, LANES), jnp.float32)
    for r in range(0, OWNERS, 2):
        slot = jnp.concatenate([slots[r : r + 1, :], slots[r + 1 : r + 2, :]], 1)
        v0 = jnp.concatenate([received[r], received[r + 1]], 1)
        a = v0.astype(jnp.bfloat16).astype(jnp.float32)
        b = (v0 - a).astype(jnp.bfloat16).astype(jnp.float32)
        c = (v0 - a) - b
        hit = jnp.broadcast_to(slot >> 7, (his, 2 * LANES)) == sub_hi
        left = jnp.concatenate(
            [jnp.where(hit, jnp.broadcast_to(v, (his, 2 * LANES)), 0.0).astype(jnp.bfloat16) for v in (a, b, c)], 0
        )
        right = jnp.where(jnp.broadcast_to(slot & 127, (LANES, 2 * LANES)) == sub_lo, 1.0, 0.0).astype(jnp.bfloat16)
        acc = acc + lax.dot_general(left, right, (((1,), (1,)), ((), ())), preferred_element_type=jnp.float32)
    out[...] = acc[0:his] + acc[his : 2 * his] + acc[2 * his : 3 * his]


def cost(us):
    return pl.CostEstimate(flops=0, bytes_accessed=int(us * 3.0e6), transcendentals=0)


def limit(mib):
    return pltpu.CompilerParams(vmem_limit_bytes=mib << 20)


F32 = jnp.float32
I32 = jnp.int32
GRID = (OWNERS, CAP)


def shape(dims, kind=F32):
    return jax.ShapeDtypeStruct(dims, kind)


def faces_call(adjoint):
    return pl.pallas_call(
        faces_kernel,
        out_shape=(shape((5, CS, NX)), shape((5, CS, NX))),
        in_specs=[HBM],
        out_specs=(VMEM, VMEM),
        scratch_shapes=[pltpu.VMEM((10, CS, 8, NX), F32), pltpu.SemaphoreType.DMA((10,))],
        compiler_params=limit(56),
        cost_estimate=cost(2),
        name="faces",
    )(adjoint)


def tables_call(cells, dirs, weight, counts, adjoint):
    return pl.pallas_call(
        tables_kernel,
        out_shape=(
            shape((PAIRS, ROWS // PAIRS, LANES)), shape((5, CV, NX)), shape((5, CV, NX)),
            shape(GRID, I32), shape(GRID, I32), shape(GRID, I32), shape(GRID),
            shape((40, LANES), I32), shape(GRID, I32),
        ),
        in_specs=[VMEM] * 4 + [HBM],
        out_specs=(HBM,) + (VMEM,) * 8,
        scratch_shapes=[
            pltpu.VMEM((Q, CS, CV, NX), F32),
            pltpu.VMEM((PAIRS, ROWS // PAIRS, LANES), F32),
            pltpu.VMEM((4, CV, NX), F32),
            pltpu.SemaphoreType.DMA((CHUNKS, N_LOAD)),
            pltpu.SemaphoreType.DMA((10,)),
            pltpu.SemaphoreType.DMA((CS,)),
        ],
        compiler_params=limit(50),
        cost_estimate=cost(8),
        name="tables",
    )(cells, dirs, weight, counts, adjoint)


SCALARS = [pltpu.SMEM((OWNERS * CAP,), I32), pltpu.SMEM((40 * LANES,), I32), pltpu.SemaphoreType.DMA((2,))]


def inner_call(ridx, list_a, lidx, pos, rim_code, table, v_up, v_dn, adjoint, saved, solid):
    return pl.pallas_call(
        inner_kernel,
        out_shape=(
            shape((Q, CS, CV, NX)), shape(GRID), shape(GRID, I32), shape(GRID, I32), shape((40, LANES), I32),
            shape((RIM_ROWS, LANES)),
        ),
        in_specs=[VMEM] * 7 + [HBM] * 4,
        out_specs=(HBM,) + (VMEM,) * 5,
        scratch_shapes=SCALARS + [
            pltpu.VMEM((ROWS, LANES), F32),
            pltpu.SemaphoreType.DMA((1,)),
            pltpu.VMEM((LISTED, 8, LANES), F32),
            pltpu.VMEM((Q, INNER, CV, NX), F32),
            pltpu.VMEM((Q, INNER, CV, NX), jnp.bfloat16),
            pltpu.VMEM((INNER, CV, NX), I32),
            pltpu.VMEM((Q, INNER, CV, NX), F32),
            pltpu.VMEM((5, COLS, CS, LANES), F32),
            pltpu.VMEM((5, COLS, CS, LANES), F32),
            pltpu.SemaphoreType.DMA((IN_CHUNKS, N_LOAD)),
            pltpu.SemaphoreType.DMA((IN_CHUNKS, 2)),
            pltpu.SemaphoreType.DMA((INNER,)),
        ],
        compiler_params=limit(50),
        cost_estimate=cost(15),
        name="inner",
    )(ridx.reshape(-1), list_a.reshape(-1), lidx, pos, rim_code, v_up, v_dn, table.reshape(ROWS, LANES), adjoint, saved, solid)


def rim_call(hidx, list_b, lidx, pos, weight, local, near, h_up, h_dn, v_up, v_dn):
    return pl.pallas_call(
        rim_kernel,
        out_shape=shape(GRID),
        in_specs=[VMEM] * 11,
        out_specs=VMEM,
        scratch_shapes=SCALARS + [pltpu.VMEM((RIM_ROWS, LANES), F32), pltpu.VMEM((LISTED, 8, LANES), F32)],
        compiler_params=limit(50),
        cost_estimate=cost(5),
        name="rim",
    )(hidx.reshape(-1), list_b.reshape(-1), lidx, pos, weight, local, near, h_up, h_dn, v_up, v_dn)


OUTER_MIB = 53


def outer_call(h_up, h_dn, v_up, v_dn, adjoint, saved, solid, recv, partial):
    return pl.pallas_call(
        outer_kernel,
        out_shape=(shape((Q, CS, CV, NX)), shape(GRID, I32)),
        in_specs=[VMEM] * 4 + [HBM] * 5,
        out_specs=(HBM, VMEM),
        scratch_shapes=[
            pltpu.VMEM((Q, 2, CV, NX), F32),
            pltpu.VMEM((Q, 2, CV, NX), jnp.bfloat16),
            pltpu.VMEM((2, CV, NX), I32),
            pltpu.VMEM((Q, 2, CV, NX), F32),
            pltpu.SemaphoreType.DMA((2, 10)),
            pltpu.SemaphoreType.DMA((2,)),
            pltpu.SemaphoreType.DMA((1,)),
        ],
        input_output_aliases={8: 0},
        compiler_params=limit(OUTER_MIB),
        cost_estimate=cost(3),
        name="outer",
    )(h_up, h_dn, v_up, v_dn, adjoint, saved, solid, recv, partial)


def sums_call(slots, received):
    return pl.pallas_call(
        sums_kernel,
        out_shape=shape((ELEM_DEV // LANES, LANES)),
        in_specs=[VMEM, VMEM],
        out_specs=VMEM,
        compiler_params=limit(16),
        cost_estimate=cost(4),
        name="element_sums",
    )(slots, received)


def body(adjoint, saved, solid, send_cells, send_dirs, send_weight, send_counts, recv_slots):
    ns = lax.axis_size("span")
    nv = lax.axis_size("vert")
    hv_up, hv_dn = faces_call(adjoint)
    v_up = lax.ppermute(hv_up, "vert", [(i, i - 1) for i in range(1, nv)])
    v_dn = lax.ppermute(hv_dn, "vert", [(i, i + 1) for i in range(nv - 1)])
    table, hs_up, hs_dn, ridx, lidx, pos, weight, list_a, rim_code = tables_call(
        send_cells[0], send_dirs[0], send_weight[0], send_counts, adjoint
    )
    hs_up = hs_up.at[1, CV - 1].set(v_up[1, 0]).at[2, 0].set(v_dn[2, 0])
    hs_dn = hs_dn.at[1, 0].set(v_dn[1, CS - 1]).at[2, CV - 1].set(v_up[2, CS - 1])
    hs_up, hs_dn, list_a = lax.optimization_barrier((hs_up, hs_dn, list_a))
    h_up = lax.ppermute(hs_up, "span", [(i, (i - 1) % ns) for i in range(ns)])
    h_dn = lax.ppermute(hs_dn, "span", [(i, (i + 1) % ns) for i in range(ns)])
    partial, local, rim_index, rim_pos, list_b, near = inner_call(
        ridx, list_a, lidx, pos, rim_code, table, v_up, v_dn, adjoint, saved, solid
    )
    values = rim_call(rim_index, list_b, lidx, rim_pos, weight, local, near, h_up, h_dn, v_up, v_dn)
    values, v_up, v_dn = lax.optimization_barrier((values, v_up, v_dn))
    received = lax.all_to_all(values[:, None, :], ("span", "vert"), split_axis=0, concat_axis=0, tiled=True)
    adjoint_prev, slots = outer_call(h_up, h_dn, v_up, v_dn, adjoint, saved, solid, recv_slots[0], partial)
    sens = sums_call(slots, received)
    return adjoint_prev, sens.reshape(ELEM_DEV)


def solution(mesh):
    return jax.shard_map(
        body,
        mesh=mesh,
        in_specs=(
            P(None, "span", "vert", None),
            P(None, "span", "vert", None),
            P("span", "vert", None),
            P(("span", "vert"), None, None),
            P(("span", "vert"), None, None),
            P(("span", "vert"), None, None),
            P(("span", "vert"), None),
            P(("span", "vert"), None, None),
        ),
        out_specs=(P(None, "span", "vert", None), P(("span", "vert"))),
        check_vma=False,
    )
```
